32 devices in a mesh: section: 2 (over x), ctx: 4 (over y, core), exp: 4 (over z).
Axes of the slice: x: 2, y: 2, z: 4, core: 2. Of those that a mesh axis runs over, the one named last changes fastest.
Arguments:
- queries: bfloat16 [4096, 1024], P('ctx', ('section', 'exp')), may hold values from -6 to 6
- key_rows: bfloat16 [4096, 1024], P('ctx', ('section', 'exp')), may hold values from -0.5 to 0.5
- value_rows: bfloat16 [4096, 1024], P('ctx', ('section', 'exp')), may hold values from -6 to 6
- gate_input: bfloat16 [4096, 1024], P('ctx', ('section', 'exp')), may hold values from -6 to 6
- norm_gain: float32 [1024], P(('section', 'exp')), may hold values from 0.25 to 1.75
- log_decay: float32 [8, 4096], P(('section', 'exp'), 'ctx'), may hold values from -1 to 0, as said below
- grad_output: bfloat16 [4096, 1024], P('ctx', ('section', 'exp')), may hold values from -6 to 6
Outputs:
- layer_out: bfloat16 [4096, 1024], P('ctx', ('section', 'exp'))
- grad_queries: bfloat16 [4096, 1024], P('ctx', ('section', 'exp'))
- grad_keys: bfloat16 [4096, 1024], P('ctx', ('section', 'exp'))
- grad_values: bfloat16 [4096, 1024], P('ctx', ('section', 'exp'))
- grad_gate: bfloat16 [4096, 1024], P('ctx', ('section', 'exp'))
The draws below stay inside these ranges and needn't reach their ends.
Inputs may be any that keep to these rules, and one draw needn't show every extreme that they name: `log_decay`: each entry is the logarithm of one head's decay factor at one position.
All inputs are finite; a program needn't handle non-finite values.
Results may differ from the reference program's by a relative error of at most 0.0051.
Values sent between devices are 32-bit elements; how exact they have to be, the bound alone decides.
A program may use at most 64 MiB of HBM per device.

```python
import math
import jax
import jax.numpy as jnp
from jax import lax

HEAD_DIM = 128
L_DEV = 1024
ATTENTION_COUNT = 8
TOKEN_SPAN = 4096


def draw_log_decay(key, part):
    keys_list = jax.random.split(jax.random.fold_in(key, 7101), 6)
    fast_share = 0.5
    is_fast = jax.random.uniform(keys_list[0], (ATTENTION_COUNT, 1)) < fast_share
    fast_rate = jnp.exp(jax.random.uniform(keys_list[1], (ATTENTION_COUNT, 1), jnp.float32, math.log(1.0 / 50.0), math.log(1.0 / 30.0)))
    slow_rate = jnp.exp(jax.random.uniform(keys_list[2], (ATTENTION_COUNT, 1), jnp.float32, math.log(0.1 / TOKEN_SPAN), math.log(0.6 / TOKEN_SPAN)))
    forgetting_factor = jnp.where(is_fast, fast_rate, slow_rate)
    approximate_guess = jax.random.uniform(keys_list[3], (ATTENTION_COUNT, TOKEN_SPAN), jnp.float32, 0.5, 2.0)
    location_array = jax.random.randint(keys_list[4], (ATTENTION_COUNT, 3), 0, TOKEN_SPAN)
    network_level = jnp.log(jax.random.uniform(keys_list[5], (ATTENTION_COUNT, 3), jnp.float32, 0.5, 0.8))
    matrix_field = jax.lax.broadcasted_iota(jnp.int32, (ATTENTION_COUNT, TOKEN_SPAN), 1)
    tile_batches = jnp.zeros((ATTENTION_COUNT, TOKEN_SPAN), jnp.float32)
    for picker_ordinal in range(3):
        tile_batches = tile_batches + jnp.where(matrix_field == location_array[:, picker_ordinal:picker_ordinal + 1], network_level[:, picker_ordinal:picker_ordinal + 1], 0.0)
    return (-forgetting_factor * approximate_guess + tile_batches).astype(jnp.float32)


def steps_of(own_key, dims, shards, low, high):
    factor_of = 1.0
    for position, blocks in shards:
        draws = jax.random.uniform(jax.random.fold_in(jax.random.fold_in(own_key, 6), position), (blocks,), jnp.float32, low / len(shards), high / len(shards))
        factor_of = factor_of * jnp.repeat(jnp.exp(draws), dims[position] // blocks).reshape((-1,) + (1,) * (len(dims) - 1 - position))
    return factor_of


def normal_values(rng, dims, spread, limit, cuts=(), held_as=jnp.bfloat16):
    array = spread * jax.random.normal(rng, dims, jnp.float32)
    if cuts:
        array = array * steps_of(rng, dims, cuts, -0.22, 0.18)
    return jnp.clip(array, -limit, limit).astype(held_as)


def setup_inputs(seed: int = 0) -> dict:
    arg_keys = jax.random.split(jax.random.key(seed), 8)
    queries = normal_values(arg_keys[0], (TOKEN_SPAN, ATTENTION_COUNT * HEAD_DIM), 1.0, 6.0, ((0, 4), (1, 8)))
    key_rows = normal_values(arg_keys[1], (TOKEN_SPAN, ATTENTION_COUNT * HEAD_DIM), HEAD_DIM ** -0.5, 0.5, ((0, 4), (1, 8)))
    value_rows = normal_values(arg_keys[2], (TOKEN_SPAN, ATTENTION_COUNT * HEAD_DIM), 1.0, 6.0, ((0, 4), (1, 8)))
    gate_input = normal_values(arg_keys[3], (TOKEN_SPAN, ATTENTION_COUNT * HEAD_DIM), 1.0, 6.0, ((0, 4), (1, 8)))
    norm_gain = jnp.clip(1.0 + 0.15 * jax.random.normal(arg_keys[4], (ATTENTION_COUNT * HEAD_DIM,), jnp.float32), 0.25, 1.75)
    log_decay = draw_log_decay(jax.random.fold_in(arg_keys[7], 71), 0)
    grad_output = normal_values(arg_keys[6], (TOKEN_SPAN, ATTENTION_COUNT * HEAD_DIM), 1.0, 6.0, ((0, 4), (1, 8)))
    return dict(queries=queries, key_rows=key_rows, value_rows=value_rows, gate_input=gate_input, norm_gain=norm_gain, log_decay=log_decay, grad_output=grad_output)


precise = lax.Precision.HIGHEST
epsilon = 1e-06

def decay_weights(log_rates):
    cumulated = jnp.cumsum(log_rates)
    length = log_rates.shape[0]
    row_index = lax.broadcasted_iota(jnp.int32, (length, length), 0)
    col_index = lax.broadcasted_iota(jnp.int32, (length, length), 1)
    lower = jnp.exp(jnp.minimum(cumulated[:, None] - cumulated[None, :], 0.0))
    return (cumulated, jnp.where(row_index >= col_index, lower, 0.0))

def block_forward(entering, pieces):
    queries, key_rows, value_rows, log_rates = pieces
    cumulated, weights_table = decay_weights(log_rates)
    scores = jnp.dot(queries, key_rows.T, preferred_element_type=jnp.float32)
    weights = (scores * weights_table).astype(jnp.bfloat16)
    carried = jnp.dot(queries.astype(jnp.float32), entering, precision=precise)
    output = jnp.dot(weights, value_rows, preferred_element_type=jnp.float32) + jnp.exp(cumulated)[:, None] * carried
    tail_decay = jnp.exp(cumulated[-1] - cumulated)[:, None]
    update = jnp.dot((key_rows.astype(jnp.float32) * tail_decay).T, value_rows.astype(jnp.float32), precision=precise)
    leaving = jnp.exp(cumulated[-1]) * entering + update
    return (leaving, (output, entering))

def split_blocks(tensor, block_len):
    return tensor.reshape((tensor.shape[0] // block_len, block_len) + tensor.shape[1:])

def forward_run(queries, key_rows, value_rows, log_rates, start, block_len):
    pieces = tuple((split_blocks(t, block_len) for t in (queries, key_rows, value_rows, log_rates)))
    closing, (outputs, entries) = lax.scan(block_forward, start, pieces)
    return (outputs.reshape(queries.shape), entries, closing)

def block_backward(leaving, pieces):
    queries, key_rows, value_rows, grad_attn, log_rates, entering = pieces
    cumulated, weights_table = decay_weights(log_rates)
    qk_weights = (jnp.dot(queries, key_rows.T, preferred_element_type=jnp.float32) * weights_table).astype(jnp.bfloat16)
    dv_weights = (jnp.dot(grad_attn, value_rows.T, preferred_element_type=jnp.float32) * weights_table).astype(jnp.bfloat16)
    front_decay = jnp.exp(cumulated)[:, None]
    tail_decay = jnp.exp(cumulated[-1] - cumulated)[:, None]
    grad_float = grad_attn.astype(jnp.float32)
    grad_q = jnp.dot(dv_weights, key_rows, preferred_element_type=jnp.float32) + front_decay * jnp.dot(grad_float, entering.T, precision=precise)
    grad_k = jnp.dot(dv_weights.T, queries, preferred_element_type=jnp.float32) + tail_decay * jnp.dot(value_rows.astype(jnp.float32), leaving.T, precision=precise)
    grad_v = jnp.dot(qk_weights.T, grad_attn, preferred_element_type=jnp.float32) + tail_decay * jnp.dot(key_rows.astype(jnp.float32), leaving, precision=precise)
    arriving = jnp.exp(cumulated[-1]) * leaving + jnp.dot((queries.astype(jnp.float32) * front_decay).T, grad_float, precision=precise)
    return (arriving, (grad_q, grad_k, grad_v))

def backward_run(queries, key_rows, value_rows, grad_attn, log_rates, entries, start, block_len):
    pieces = tuple((split_blocks(t, block_len) for t in (queries, key_rows, value_rows, grad_attn, log_rates))) + (entries,)
    closing, (grad_q, grad_k, grad_v) = lax.scan(block_backward, start, pieces, reverse=True)
    shape = queries.shape
    return (grad_q.reshape(shape), grad_k.reshape(shape), grad_v.reshape(shape), closing)

def by_heads(tensor, head_count):
    return tensor.reshape(tensor.shape[0], head_count, HEAD_DIM).transpose(1, 0, 2)

def from_heads(tensor):
    return tensor.transpose(1, 0, 2).reshape(tensor.shape[1], tensor.shape[0] * tensor.shape[2])

def reference(queries, key_rows, value_rows, gate_input, norm_gain, log_decay, grad_output):
    block_len = min(512, L_DEV)
    head_count = log_decay.shape[0]
    total_width = head_count * HEAD_DIM
    zero_state = jnp.zeros((HEAD_DIM, HEAD_DIM), jnp.float32)
    query_heads = by_heads(queries, head_count)
    key_heads = by_heads(key_rows, head_count)
    value_heads = by_heads(value_rows, head_count)

    def forward_head(items):
        outputs, entries, closing = forward_run(items[0], items[1], items[2], items[3], zero_state, block_len)
        return (outputs, entries)
    attn_heads, entries = lax.map(forward_head, (query_heads, key_heads, value_heads, log_decay))
    full_out = from_heads(attn_heads)
    squares = lax.optimization_barrier(jnp.sum(full_out * full_out, axis=1))
    inv_rms = lax.rsqrt(squares / total_width + epsilon)
    normed = full_out * inv_rms[:, None]
    gate_prob = jax.nn.sigmoid(gate_input.astype(jnp.float32))
    scaled = normed * norm_gain
    layer_out = (scaled * gate_prob).astype(jnp.bfloat16)
    grad_float = grad_output.astype(jnp.float32)
    grad_gate = (grad_float * scaled * gate_prob * (1.0 - gate_prob)).astype(jnp.bfloat16)
    signal = grad_float * gate_prob * norm_gain
    along = lax.optimization_barrier(jnp.sum(signal * normed, axis=1)) / total_width
    grad_attn = (inv_rms[:, None] * (signal - normed * along[:, None])).astype(jnp.bfloat16)
    grad_heads = by_heads(grad_attn, head_count)

    def backward_head(items):
        grad_q, grad_k, grad_v, closing = backward_run(items[0], items[1], items[2], items[3], items[4], items[5], zero_state, block_len)
        return (grad_q, grad_k, grad_v)
    grad_q, grad_k, grad_v = lax.map(backward_head, (query_heads, key_heads, value_heads, grad_heads, log_decay, entries))
    return (layer_out, from_heads(grad_q).astype(jnp.bfloat16), from_heads(grad_k).astype(jnp.bfloat16), from_heads(grad_v).astype(jnp.bfloat16), grad_gate)
```

```python
from functools import partial

import jax
import jax.numpy as jnp
from jax import lax
from jax.experimental import pallas as pl
from jax.experimental.pallas import tpu as pltpu
from jax.sharding import PartitionSpec as P

MESH = pl.DeviceIdType.MESH
BF = jnp.bfloat16
F32 = jnp.float32
epsilon = 1e-06
EXTRA = 8

NN = (((1,), (0,)), ((), ()))
NT = (((1,), (1,)), ((), ()))
TN = (((0,), (0,)), ((), ()))


def mm(a, b, dims):
    return lax.dot_general(a, b, dims, preferred_element_type=F32)


def split(x):
    high = x.astype(BF)
    return high, (x - high.astype(F32)).astype(BF)


def prefix_rows(x):
    lane = lax.broadcasted_iota(jnp.int32, x.shape, 1)
    shift = 1
    while shift < x.shape[1]:
        x = x + jnp.where(lane >= shift, pltpu.roll(x, shift, 1), 0.0)
        shift *= 2
    return x


def kernel(
    sizes,
    q_h, k_h, v_h, gi_h, go_h, gain_ref, ld_ref,
    lo_h, gq_h, gk_h, gv_h, gg_h,
    q, k, v, gi, go, lo, gq, gk, gv, gg,
    steps, fd, tail, table, wq, attn, signal, gate, upd, ent, g, gkl, gvl,
    fsend, frecv, bsend, brecv, acc, rsend, rrecv, coef,
    in_sem, out_sem, fs_sem, fr_sem, bs_sem, br_sem, rs_sem, rr_sem,
):
    n_ctx, n_sec, n_exp, chunk = sizes
    n_norm = n_sec * n_exp
    length, dim = q.shape
    count = length // chunk
    me = lax.axis_index("ctx")
    sec = lax.axis_index("section")
    ex = lax.axis_index("exp")
    mine = sec * n_exp + ex
    width = float(dim * n_norm)

    def norm_peer(r):
        other = lax.rem(mine + r, n_norm)
        return {"section": lax.div(other, n_exp), "exp": lax.rem(other, n_exp)}

    barrier = pltpu.get_barrier_semaphore()
    for r in range(1, n_ctx):
        pl.semaphore_signal(
            barrier, inc=1, device_id={"ctx": lax.rem(me + r, n_ctx)}, device_id_type=MESH
        )
    for r in range(1, n_norm):
        pl.semaphore_signal(barrier, inc=1, device_id=norm_peer(r), device_id_type=MESH)

    loads = [
        pltpu.make_async_copy(src, dst, in_sem.at[i])
        for i, (src, dst) in enumerate(
            ((k_h, k), (v_h, v), (q_h, q), (gi_h, gi), (go_h, go))
        )
    ]
    for copy in loads:
        copy.start()
    stores = [
        pltpu.make_async_copy(src, dst, out_sem.at[i])
        for i, (src, dst) in enumerate(
            ((lo, lo_h), (gg, gg_h), (gq, gq_h), (gk, gk_h), (gv, gv_h))
        )
    ]

    rows = [pl.ds(c * chunk, chunk) for c in range(count)]

    steps[...] = jnp.zeros_like(steps)
    for c in range(count):
        steps[c : c + 1, :] = ld_ref[:, c * chunk : (c + 1) * chunk]
    run = prefix_rows(steps[...])
    steps[...] = run
    run_t = jnp.transpose(run)
    ends = [run[c : c + 1, chunk - 1 : chunk] for c in range(count)]
    for c in range(count):
        column = jnp.broadcast_to(run_t[:, c : c + 1], (chunk, dim))
        fd[rows[c], :] = jnp.exp(column)
        tail[rows[c], :] = jnp.exp(ends[c] - column)

    loads[0].wait()
    loads[1].wait()
    local = None
    total = None
    for c in range(count):
        high, low = split(k[rows[c], :].astype(F32) * tail[rows[c], :])
        vc = v[rows[c], :]
        update = mm(high, vc, TN) + mm(low, vc, TN)
        upd[c] = update
        local = update if local is None else jnp.exp(ends[c]) * local + update
        total = ends[c] if total is None else total + ends[c]
    fsend[0:dim, :] = local
    fsend[dim : dim + EXTRA, :] = jnp.broadcast_to(total, (EXTRA, dim))

    pl.semaphore_wait(barrier, n_ctx - 1 + n_norm - 1)

    def forward_copy(r):
        return pltpu.make_async_remote_copy(
            src_ref=fsend, dst_ref=frecv.at[r], send_sem=fs_sem.at[r], recv_sem=fr_sem.at[r],
            device_id={"ctx": lax.rem(me + r, n_ctx)}, device_id_type=MESH,
        )

    def backward_copy(r):
        return pltpu.make_async_remote_copy(
            src_ref=bsend, dst_ref=brecv.at[r], send_sem=bs_sem.at[r], recv_sem=br_sem.at[r],
            device_id={"ctx": lax.rem(me + n_ctx - r, n_ctx)}, device_id_type=MESH,
        )

    def row_copy(r):
        return pltpu.make_async_remote_copy(
            src_ref=rsend, dst_ref=rrecv.at[r], send_sem=rs_sem.at[r], recv_sem=rr_sem.at[r],
            device_id=norm_peer(r), device_id_type=MESH,
        )

    for r in range(1, n_ctx):
        @pl.when(me + r < n_ctx)
        def _(r=r):
            forward_copy(r).start()

    loads[2].wait()
    t_index = lax.broadcasted_iota(jnp.int32, (chunk, chunk), 0)
    s_index = lax.broadcasted_iota(jnp.int32, (chunk, chunk), 1)
    for c in range(count):
        column = jnp.broadcast_to(run_t[:, c : c + 1], (chunk, chunk))
        gap = jnp.minimum(column - steps[c : c + 1, :], 0.0)
        weights = jnp.where(t_index >= s_index, jnp.exp(gap), 0.0)
        table[c] = weights
        scores = (mm(q[rows[c], :], k[rows[c], :], NT) * weights).astype(BF)
        wq[c] = scores
        attn[rows[c], :] = mm(scores, v[rows[c], :], NN)
    loads[3].wait()
    loads[4].wait()
    gain = gain_ref[...]
    for c in range(count):
        prob = jax.nn.sigmoid(gi[rows[c], :].astype(F32))
        gate[rows[c], :] = prob
        signal[rows[c], :] = go[rows[c], :].astype(F32) * prob * gain

    acc[...] = jnp.zeros_like(acc)
    for r in range(n_ctx - 1, 0, -1):
        @pl.when(me >= r)
        def _(r=r):
            forward_copy(r).wait_recv()
            acc[...] = jnp.exp(frecv[r, dim : dim + 1, :]) * acc[...] + frecv[r, 0:dim, :]

    state = acc[...]
    ones = jnp.ones((8, dim), BF)
    for c in range(count):
        high, low = split(state)
        ent[c, :, 0:dim] = high
        ent[c, :, dim : 2 * dim] = low
        both = mm(q[rows[c], :], ent[c], NN)
        full = attn[rows[c], :] + fd[rows[c], :] * (both[:, 0:dim] + both[:, dim : 2 * dim])
        attn[rows[c], :] = full
        rsend[0:1, rows[c]] = mm(ones, (full * full).astype(BF), NT)[0:1, :]
        rsend[1:2, rows[c]] = mm(ones, (signal[rows[c], :] * full).astype(BF), NT)[0:1, :]
        if c + 1 < count:
            state = jnp.exp(ends[c]) * state + upd[c]

    for r in range(1, n_norm):
        row_copy(r).start()
    coef[...] = jnp.zeros_like(coef)
    sums = rsend[...]
    for r in range(1, n_norm):
        row_copy(r).wait_recv()
        sums = sums + rrecv[r]
    inv = lax.rsqrt(sums[0:1, :] / width + epsilon)
    coef[0:1, :] = inv
    coef[1:2, :] = inv * inv * (sums[1:2, :] / width)

    seen = [None] * count
    for c in range(count):
        turned = jnp.transpose(coef[:, rows[c]])
        inv_b = jnp.broadcast_to(turned[:, 0:1], (chunk, dim))
        along_b = jnp.broadcast_to(turned[:, 1:2], (chunk, dim))
        full = attn[rows[c], :]
        grad = (inv_b * (signal[rows[c], :] - full * along_b)).astype(BF)
        g[rows[c], :] = grad
        high, low = split(q[rows[c], :].astype(F32) * fd[rows[c], :])
        seen[c] = mm(high, grad, TN) + mm(low, grad, TN)
        upd[c] = seen[c]
        scaled = full * inv_b * gain
        prob = gate[rows[c], :]
        out = scaled * prob
        lo[rows[c], :] = out.astype(BF)
        gg[rows[c], :] = (go[rows[c], :].astype(F32) * out * (1.0 - prob)).astype(BF)
    local = None
    for c in range(count - 1, -1, -1):
        local = seen[c] if local is None else jnp.exp(ends[c]) * local + seen[c]
    bsend[0:dim, :] = local
    bsend[dim : dim + EXTRA, :] = jnp.broadcast_to(total, (EXTRA, dim))
    for r in range(1, n_ctx):
        @pl.when(me >= r)
        def _(r=r):
            backward_copy(r).start()
    stores[0].start()
    stores[1].start()

    for c in range(count):
        grad = g[rows[c], :]
        dv = (mm(grad, v[rows[c], :], NT) * table[c]).astype(BF)
        high = mm(grad, ent[c, :, 0:dim], NT)
        low = mm(grad, ent[c, :, dim : 2 * dim], NT)
        gq[rows[c], :] = (
            mm(dv, k[rows[c], :], NN) + fd[rows[c], :] * (high + low)
        ).astype(BF)
        gkl[rows[c], :] = mm(dv, q[rows[c], :], TN)
        gvl[rows[c], :] = mm(wq[c], grad, TN)
    stores[2].start()

    acc[...] = jnp.zeros_like(acc)
    for r in range(n_ctx - 1, 0, -1):
        @pl.when(me + r < n_ctx)
        def _(r=r):
            backward_copy(r).wait_recv()
            acc[...] = jnp.exp(brecv[r, dim : dim + 1, :]) * acc[...] + brecv[r, 0:dim, :]

    state = acc[...]
    for c in range(count - 1, -1, -1):
        high, low = split(state)
        fall = tail[rows[c], :]
        vc = v[rows[c], :]
        kc = k[rows[c], :]
        gk[rows[c], :] = (gkl[rows[c], :] + fall * (mm(vc, high, NT) + mm(vc, low, NT))).astype(BF)
        gv[rows[c], :] = (gvl[rows[c], :] + fall * (mm(kc, high, NN) + mm(kc, low, NN))).astype(BF)
        if c > 0:
            state = jnp.exp(ends[c]) * state + upd[c]
    stores[3].start()
    stores[4].start()

    for r in range(1, n_ctx):
        @pl.when(me + r < n_ctx)
        def _(r=r):
            forward_copy(r).wait_send()

        @pl.when(me >= r)
        def _(r=r):
            backward_copy(r).wait_send()
    for r in range(1, n_norm):
        row_copy(r).wait_send()
    for copy in stores:
        copy.wait()


def on_device(n_ctx, n_sec, n_exp, queries, key_rows, value_rows, gate_input, norm_gain, log_decay, grad_output):
    length, dim = queries.shape
    assert log_decay.shape[0] == 1
    chunk = min(256, length)
    count = length // chunk
    assert count * chunk == length and count <= 8
    n_norm = n_sec * n_exp
    any_spec = pl.BlockSpec(memory_space=pl.ANY)
    vmem_spec = pl.BlockSpec(memory_space=pltpu.VMEM)
    block = lambda dtype: pltpu.VMEM((length, dim), dtype)
    sem = lambda n: pltpu.SemaphoreType.DMA((n,))
    return pl.pallas_call(
        partial(kernel, (n_ctx, n_sec, n_exp, chunk)),
        out_shape=[jax.ShapeDtypeStruct((length, dim), BF)] * 5,
        in_specs=[any_spec] * 5 + [vmem_spec] * 2,
        out_specs=[any_spec] * 5,
        scratch_shapes=[block(BF)] * 10
        + [
            pltpu.VMEM((8, chunk), F32),
            block(F32),
            block(F32),
            pltpu.VMEM((count, chunk, chunk), F32),
            pltpu.VMEM((count, chunk, chunk), BF),
            block(F32),
            block(F32),
            block(F32),
            pltpu.VMEM((count, dim, dim), F32),
            pltpu.VMEM((count, dim, 2 * dim), BF),
            block(BF),
            block(F32),
            block(F32),
            pltpu.VMEM((dim + EXTRA, dim), F32),
            pltpu.VMEM((n_ctx, dim + EXTRA, dim), F32),
            pltpu.VMEM((dim + EXTRA, dim), F32),
            pltpu.VMEM((n_ctx, dim + EXTRA, dim), F32),
            pltpu.VMEM((dim, dim), F32),
            pltpu.VMEM((2, length), F32),
            pltpu.VMEM((n_norm, 2, length), F32),
            pltpu.VMEM((8, length), F32),
            sem(5), sem(5), sem(n_ctx), sem(n_ctx), sem(n_ctx), sem(n_ctx), sem(n_norm), sem(n_norm),
        ],
        compiler_params=pltpu.CompilerParams(
            collective_id=0, has_side_effects=True, vmem_limit_bytes=48 * 1024 * 1024
        ),
    )(queries, key_rows, value_rows, gate_input, grad_output, norm_gain.reshape(1, dim), log_decay)


def solution(mesh):
    rows = P("ctx", ("section", "exp"))
    in_specs = (rows, rows, rows, rows, P(("section", "exp")), P(("section", "exp"), "ctx"), rows)
    call = partial(on_device, mesh.shape["ctx"], mesh.shape["section"], mesh.shape["exp"])

    def run(*args):
        return tuple(call(*args))

    return jax.shard_map(run, mesh=mesh, in_specs=in_specs, out_specs=(rows,) * 5, check_vma=False)
```

```python
from functools import partial

import jax
import jax.numpy as jnp
from jax import lax
from jax.experimental import pallas as pl
from jax.experimental.pallas import tpu as pltpu
from jax.sharding import PartitionSpec as P

MESH = pl.DeviceIdType.MESH
BF = jnp.bfloat16
F32 = jnp.float32
epsilon = 1e-06
EXTRA = 8

NN = (((1,), (0,)), ((), ()))
NT = (((1,), (1,)), ((), ()))
TN = (((0,), (0,)), ((), ()))


def mm(a, b, dims):
    return lax.dot_general(a, b, dims, preferred_element_type=F32)


def split(x):
    high = x.astype(BF)
    return high, (x - high.astype(F32)).astype(BF)


def prefix_rows(x):
    lane = lax.broadcasted_iota(jnp.int32, x.shape, 1)
    shift = 1
    while shift < x.shape[1]:
        x = x + jnp.where(lane >= shift, pltpu.roll(x, shift, 1), 0.0)
        shift *= 2
    return x


def kernel(
    sizes,
    q_h, k_h, v_h, gi_h, go_h, gain_h, ld_h,
    lo_h, gq_h, gk_h, gv_h, gg_h,
    q, k, v, gi, go, lo, gq, gk, gv, gg,
    gain_ref, ld_ref, steps, fd, tail, table, wq, attn, signal, gate, upd, ent, g, gkl, gvl,
    fsend, frecv, bsend, brecv, acc, rsend, rrecv, coef,
    in_sem, out_sem, fs_sem, fr_sem, bs_sem, br_sem, rs_sem, rr_sem,
):
    n_ctx, n_sec, n_exp, chunk = sizes
    n_norm = n_sec * n_exp
    length, dim = q.shape
    count = length // chunk
    me = lax.axis_index("ctx")
    sec = lax.axis_index("section")
    ex = lax.axis_index("exp")
    mine = sec * n_exp + ex
    width = float(dim * n_norm)

    def norm_peer(r):
        other = lax.rem(mine + r, n_norm)
        return {"section": lax.div(other, n_exp), "exp": lax.rem(other, n_exp)}

    loads = [
        pltpu.make_async_copy(src, dst, in_sem.at[i])
        for i, (src, dst) in enumerate(
            ((k_h, k), (v_h, v), (q_h, q), (gi_h, gi), (go_h, go), (gain_h, gain_ref), (ld_h, ld_ref))
        )
    ]
    for i in (6, 0, 1, 2, 3, 4, 5):
        loads[i].start()

    barrier = pltpu.get_barrier_semaphore()
    for r in range(1, n_ctx):
        pl.semaphore_signal(
            barrier, inc=1, device_id={"ctx": lax.rem(me + r, n_ctx)}, device_id_type=MESH
        )
    for r in range(1, n_norm):
        pl.semaphore_signal(barrier, inc=1, device_id=norm_peer(r), device_id_type=MESH)

    stores = [
        pltpu.make_async_copy(src, dst, out_sem.at[i])
        for i, (src, dst) in enumerate(
            ((lo, lo_h), (gg, gg_h), (gq, gq_h), (gk, gk_h), (gv, gv_h))
        )
    ]

    rows = [pl.ds(c * chunk, chunk) for c in range(count)]

    steps[...] = jnp.zeros_like(steps)
    loads[6].wait()
    for c in range(count):
        steps[c : c + 1, :] = ld_ref[:, c * chunk : (c + 1) * chunk]
    run = prefix_rows(steps[...])
    steps[...] = run
    run_t = jnp.transpose(run)
    ends = [run[c : c + 1, chunk - 1 : chunk] for c in range(count)]
    for c in range(count):
        column = jnp.broadcast_to(run_t[:, c : c + 1], (chunk, dim))
        fd[rows[c], :] = jnp.exp(column)
        tail[rows[c], :] = jnp.exp(ends[c] - column)

    loads[0].wait()
    loads[1].wait()
    local = None
    total = None
    for c in range(count):
        high, low = split(k[rows[c], :].astype(F32) * tail[rows[c], :])
        vc = v[rows[c], :]
        update = mm(high, vc, TN) + mm(low, vc, TN)
        upd[c] = update
        local = update if local is None else jnp.exp(ends[c]) * local + update
        total = ends[c] if total is None else total + ends[c]
    fsend[0:dim, :] = local
    fsend[dim : dim + EXTRA, :] = jnp.broadcast_to(total, (EXTRA, dim))

    pl.semaphore_wait(barrier, n_ctx - 1 + n_norm - 1)

    def forward_copy(r):
        return pltpu.make_async_remote_copy(
            src_ref=fsend, dst_ref=frecv.at[r], send_sem=fs_sem.at[r], recv_sem=fr_sem.at[r],
            device_id={"ctx": lax.rem(me + r, n_ctx)}, device_id_type=MESH,
        )

    def backward_copy(r):
        return pltpu.make_async_remote_copy(
            src_ref=bsend, dst_ref=brecv.at[r], send_sem=bs_sem.at[r], recv_sem=br_sem.at[r],
            device_id={"ctx": lax.rem(me + n_ctx - r, n_ctx)}, device_id_type=MESH,
        )

    def row_copy(r):
        return pltpu.make_async_remote_copy(
            src_ref=rsend, dst_ref=rrecv.at[r], send_sem=rs_sem.at[r], recv_sem=rr_sem.at[r],
            device_id=norm_peer(r), device_id_type=MESH,
        )

    for r in range(1, n_ctx):
        @pl.when(me + r < n_ctx)
        def _(r=r):
            forward_copy(r).start()

    loads[2].wait()
    t_index = lax.broadcasted_iota(jnp.int32, (chunk, chunk), 0)
    s_index = lax.broadcasted_iota(jnp.int32, (chunk, chunk), 1)
    for c in range(count):
        column = jnp.broadcast_to(run_t[:, c : c + 1], (chunk, chunk))
        gap = jnp.minimum(column - steps[c : c + 1, :], 0.0)
        weights = jnp.where(t_index >= s_index, jnp.exp(gap), 0.0)
        table[c] = weights
        scores = (mm(q[rows[c], :], k[rows[c], :], NT) * weights).astype(BF)
        wq[c] = scores
        attn[rows[c], :] = mm(scores, v[rows[c], :], NN)
    loads[3].wait()
    loads[4].wait()
    loads[5].wait()
    gain = gain_ref[...]
    for c in range(count):
        prob = jax.nn.sigmoid(gi[rows[c], :].astype(F32))
        gate[rows[c], :] = prob
        signal[rows[c], :] = go[rows[c], :].astype(F32) * prob * gain

    acc[...] = jnp.zeros_like(acc)
    for r in range(n_ctx - 1, 0, -1):
        @pl.when(me >= r)
        def _(r=r):
            forward_copy(r).wait_recv()
            acc[...] = jnp.exp(frecv[r, dim : dim + 1, :]) * acc[...] + frecv[r, 0:dim, :]

    state = acc[...]
    ones = jnp.ones((8, dim), BF)
    for c in range(count):
        high, low = split(state)
        ent[c, :, 0:dim] = high
        ent[c, :, dim : 2 * dim] = low
        both = mm(q[rows[c], :], ent[c], NN)
        full = attn[rows[c], :] + fd[rows[c], :] * (both[:, 0:dim] + both[:, dim : 2 * dim])
        attn[rows[c], :] = full
        rsend[0:1, rows[c]] = mm(ones, (full * full).astype(BF), NT)[0:1, :]
        rsend[1:2, rows[c]] = mm(ones, (signal[rows[c], :] * full).astype(BF), NT)[0:1, :]
        if c + 1 < count:
            state = jnp.exp(ends[c]) * state + upd[c]

    for r in range(1, n_norm):
        row_copy(r).start()
    coef[...] = jnp.zeros_like(coef)
    sums = rsend[...]
    for r in range(1, n_norm):
        row_copy(r).wait_recv()
        sums = sums + rrecv[r]
    inv = lax.rsqrt(sums[0:1, :] / width + epsilon)
    coef[0:1, :] = inv
    coef[1:2, :] = inv * inv * (sums[1:2, :] / width)

    seen = [None] * count
    for c in range(count):
        turned = jnp.transpose(coef[:, rows[c]])
        inv_b = jnp.broadcast_to(turned[:, 0:1], (chunk, dim))
        along_b = jnp.broadcast_to(turned[:, 1:2], (chunk, dim))
        full = attn[rows[c], :]
        grad = (inv_b * (signal[rows[c], :] - full * along_b)).astype(BF)
        g[rows[c], :] = grad
        high, low = split(q[rows[c], :].astype(F32) * fd[rows[c], :])
        seen[c] = mm(high, grad, TN) + mm(low, grad, TN)
        upd[c] = seen[c]
        scaled = full * inv_b * gain
        prob = gate[rows[c], :]
        out = scaled * prob
        lo[rows[c], :] = out.astype(BF)
        gg[rows[c], :] = (go[rows[c], :].astype(F32) * out * (1.0 - prob)).astype(BF)
    local = None
    for c in range(count - 1, -1, -1):
        local = seen[c] if local is None else jnp.exp(ends[c]) * local + seen[c]
    bsend[0:dim, :] = local
    bsend[dim : dim + EXTRA, :] = jnp.broadcast_to(total, (EXTRA, dim))
    for r in range(1, n_ctx):
        @pl.when(me >= r)
        def _(r=r):
            backward_copy(r).start()
    stores[0].start()
    stores[1].start()

    for c in range(count):
        grad = g[rows[c], :]
        dv = (mm(grad, v[rows[c], :], NT) * table[c]).astype(BF)
        high = mm(grad, ent[c, :, 0:dim], NT)
        low = mm(grad, ent[c, :, dim : 2 * dim], NT)
        gq[rows[c], :] = (
            mm(dv, k[rows[c], :], NN) + fd[rows[c], :] * (high + low)
        ).astype(BF)
        gkl[rows[c], :] = mm(dv, q[rows[c], :], TN)
        gvl[rows[c], :] = mm(wq[c], grad, TN)
    stores[2].start()

    acc[...] = jnp.zeros_like(acc)
    for r in range(n_ctx - 1, 0, -1):
        @pl.when(me + r < n_ctx)
        def _(r=r):
            backward_copy(r).wait_recv()
            acc[...] = jnp.exp(brecv[r, dim : dim + 1, :]) * acc[...] + brecv[r, 0:dim, :]

    state = acc[...]
    for c in range(count - 1, -1, -1):
        high, low = split(state)
        fall = tail[rows[c], :]
        vc = v[rows[c], :]
        kc = k[rows[c], :]
        gk[rows[c], :] = (gkl[rows[c], :] + fall * (mm(vc, high, NT) + mm(vc, low, NT))).astype(BF)
        gv[rows[c], :] = (gvl[rows[c], :] + fall * (mm(kc, high, NN) + mm(kc, low, NN))).astype(BF)
        if c > 0:
            state = jnp.exp(ends[c]) * state + upd[c]
    stores[3].start()
    stores[4].start()

    for r in range(1, n_ctx):
        @pl.when(me + r < n_ctx)
        def _(r=r):
            forward_copy(r).wait_send()

        @pl.when(me >= r)
        def _(r=r):
            backward_copy(r).wait_send()
    for r in range(1, n_norm):
        row_copy(r).wait_send()
    for copy in stores:
        copy.wait()


def hand_out(*refs):
    copies = [pltpu.make_async_copy(refs[i], refs[5 + i], refs[10].at[i]) for i in range(5)]
    for copy in copies:
        copy.start()
    for copy in copies:
        copy.wait()


def on_device(n_ctx, n_sec, n_exp, queries, key_rows, value_rows, gate_input, norm_gain, log_decay, grad_output):
    length, dim = queries.shape
    assert log_decay.shape[0] == 1
    chunk = min(256, length)
    count = length // chunk
    assert count * chunk == length and count <= 8
    n_norm = n_sec * n_exp
    any_spec = pl.BlockSpec(memory_space=pl.ANY)
    hbm_spec = pl.BlockSpec(memory_space=pltpu.HBM)
    block = lambda dtype: pltpu.VMEM((length, dim), dtype)
    sem = lambda n: pltpu.SemaphoreType.DMA((n,))
    results = pl.pallas_call(
        partial(kernel, (n_ctx, n_sec, n_exp, chunk)),
        out_shape=[jax.ShapeDtypeStruct((length, dim), BF)] * 5,
        in_specs=[hbm_spec] * 7,
        out_specs=[any_spec] * 5,
        scratch_shapes=[block(BF)] * 10
        + [
            pltpu.VMEM((1, dim), F32),
            pltpu.VMEM((1, length), F32),
            pltpu.VMEM((8, chunk), F32),
            block(F32),
            block(F32),
            pltpu.VMEM((count, chunk, chunk), F32),
            pltpu.VMEM((count, chunk, chunk), BF),
            block(F32),
            block(F32),
            block(F32),
            pltpu.VMEM((count, dim, dim), F32),
            pltpu.VMEM((count, dim, 2 * dim), BF),
            block(BF),
            block(F32),
            block(F32),
            pltpu.VMEM((dim + EXTRA, dim), F32),
            pltpu.VMEM((n_ctx, dim + EXTRA, dim), F32),
            pltpu.VMEM((dim + EXTRA, dim), F32),
            pltpu.VMEM((n_ctx, dim + EXTRA, dim), F32),
            pltpu.VMEM((dim, dim), F32),
            pltpu.VMEM((2, length), F32),
            pltpu.VMEM((n_norm, 2, length), F32),
            pltpu.VMEM((8, length), F32),
            sem(7), sem(5), sem(n_ctx), sem(n_ctx), sem(n_ctx), sem(n_ctx), sem(n_norm), sem(n_norm),
        ],
        compiler_params=pltpu.CompilerParams(
            collective_id=0, has_side_effects=True, vmem_limit_bytes=48 * 1024 * 1024
        ),
    )(*[
        pltpu.with_memory_space_constraint(x, pltpu.HBM)
        for x in (queries, key_rows, value_rows, gate_input, grad_output, norm_gain.reshape(1, dim), log_decay)
    ])
    return pl.pallas_call(
        hand_out,
        out_shape=[jax.ShapeDtypeStruct((length, dim), BF)] * 5,
        in_specs=[any_spec] * 5,
        out_specs=[hbm_spec] * 5,
        scratch_shapes=[sem(5)],
    )(*results)


def solution(mesh):
    rows = P("ctx", ("section", "exp"))
    in_specs = (rows, rows, rows, rows, P(("section", "exp")), P(("section", "exp"), "ctx"), rows)
    call = partial(on_device, mesh.shape["ctx"], mesh.shape["section"], mesh.shape["exp"])

    def run(*args):
        return tuple(call(*args))

    return jax.shard_map(run, mesh=mesh, in_specs=in_specs, out_specs=(rows,) * 5, check_vma=False)
```

```python
from functools import partial

import jax
import jax.numpy as jnp
from jax import lax
from jax.experimental import pallas as pl
from jax.experimental.pallas import tpu as pltpu
from jax.sharding import PartitionSpec as P

MESH = pl.DeviceIdType.MESH
BF = jnp.bfloat16
F32 = jnp.float32
epsilon = 1e-06
EXTRA = 8

NN = (((1,), (0,)), ((), ()))
NT = (((1,), (1,)), ((), ()))
TN = (((0,), (0,)), ((), ()))


def mm(a, b, dims):
    return lax.dot_general(a, b, dims, preferred_element_type=F32)


def split(x):
    high = x.astype(BF)
    return high, (x - high.astype(F32)).astype(BF)


def prefix_rows(x):
    lane = lax.broadcasted_iota(jnp.int32, x.shape, 1)
    shift = 1
    while shift < x.shape[1]:
        x = x + jnp.where(lane >= shift, pltpu.roll(x, shift, 1), 0.0)
        shift *= 2
    return x


def kernel(
    sizes,
    q_h, k_h, v_h, gi_h, go_h, gain_h, ld_h,
    lo_h, gq_h, gk_h, gv_h, gg_h,
    q, k, v, gi, go, lo, gq, gk, gv, gg,
    gain_ref, ld_ref, steps, fd, tail, table, wq, attn, signal, gate, upd, ent, g, gkl, gvl,
    fsend, frecv, bsend, brecv, acc, rsend, rrecv, coef,
    in_sem, out_sem, fs_sem, fr_sem, bs_sem, br_sem, rs_sem, rr_sem,
):
    n_ctx, n_sec, n_exp, chunk = sizes
    n_norm = n_sec * n_exp
    length, dim = q.shape
    count = length // chunk
    me = lax.axis_index("ctx")
    sec = lax.axis_index("section")
    ex = lax.axis_index("exp")
    mine = sec * n_exp + ex
    width = float(dim * n_norm)

    def norm_peer(r):
        other = lax.rem(mine + r, n_norm)
        return {"section": lax.div(other, n_exp), "exp": lax.rem(other, n_exp)}

    loads = [
        pltpu.make_async_copy(src, dst, in_sem.at[i])
        for i, (src, dst) in enumerate(
            ((k_h, k), (v_h, v), (q_h, q), (gi_h, gi), (go_h, go), (gain_h, gain_ref), (ld_h, ld_ref))
        )
    ]
    for i in (6, 0, 1, 2, 3, 4, 5):
        loads[i].start()

    barrier = pltpu.get_barrier_semaphore()
    for r in range(1, n_ctx):
        pl.semaphore_signal(
            barrier, inc=1, device_id={"ctx": lax.rem(me + r, n_ctx)}, device_id_type=MESH
        )
    for r in range(1, n_norm):
        pl.semaphore_signal(barrier, inc=1, device_id=norm_peer(r), device_id_type=MESH)

    stores = [
        pltpu.make_async_copy(src, dst, out_sem.at[i])
        for i, (src, dst) in enumerate(
            ((lo, lo_h), (gg, gg_h), (gq, gq_h), (gk, gk_h), (gv, gv_h))
        )
    ]

    rows = [pl.ds(c * chunk, chunk) for c in range(count)]

    steps[...] = jnp.zeros_like(steps)
    loads[6].wait()
    for c in range(count):
        steps[c : c + 1, :] = ld_ref[:, c * chunk : (c + 1) * chunk]
    run = prefix_rows(steps[...])
    steps[...] = run
    run_t = jnp.transpose(run)
    ends = [run[c : c + 1, chunk - 1 : chunk] for c in range(count)]
    for c in range(count):
        column = jnp.broadcast_to(run_t[:, c : c + 1], (chunk, dim))
        fd[rows[c], :] = jnp.exp(column)
        tail[rows[c], :] = jnp.exp(ends[c] - column)

    loads[0].wait()
    loads[1].wait()
    local = None
    total = None
    for c in range(count):
        high, low = split(k[rows[c], :].astype(F32) * tail[rows[c], :])
        vc = v[rows[c], :]
        update = mm(high, vc, TN) + mm(low, vc, TN)
        upd[c] = update
        local = update if local is None else jnp.exp(ends[c]) * local + update
        total = ends[c] if total is None else total + ends[c]
    fsend[0:dim, :] = local
    fsend[dim : dim + EXTRA, :] = jnp.broadcast_to(total, (EXTRA, dim))

    pl.semaphore_wait(barrier, n_ctx - 1 + n_norm - 1)

    def forward_copy(r):
        return pltpu.make_async_remote_copy(
            src_ref=fsend, dst_ref=frecv.at[r], send_sem=fs_sem.at[r], recv_sem=fr_sem.at[r],
            device_id={"ctx": lax.rem(me + r, n_ctx)}, device_id_type=MESH,
        )

    def backward_copy(r):
        return pltpu.make_async_remote_copy(
            src_ref=bsend, dst_ref=brecv.at[r], send_sem=bs_sem.at[r], recv_sem=br_sem.at[r],
            device_id={"ctx": lax.rem(me + n_ctx - r, n_ctx)}, device_id_type=MESH,
        )

    def row_copy(r):
        return pltpu.make_async_remote_copy(
            src_ref=rsend, dst_ref=rrecv.at[r], send_sem=rs_sem.at[r], recv_sem=rr_sem.at[r],
            device_id=norm_peer(r), device_id_type=MESH,
        )

    for r in range(1, n_ctx):
        @pl.when(me + r < n_ctx)
        def _(r=r):
            forward_copy(r).start()

    loads[2].wait()
    t_index = lax.broadcasted_iota(jnp.int32, (chunk, chunk), 0)
    s_index = lax.broadcasted_iota(jnp.int32, (chunk, chunk), 1)
    for c in range(count):
        column = jnp.broadcast_to(run_t[:, c : c + 1], (chunk, chunk))
        gap = jnp.minimum(column - steps[c : c + 1, :], 0.0)
        weights = jnp.where(t_index >= s_index, jnp.exp(gap), 0.0)
        table[c] = weights
        scores = (mm(q[rows[c], :], k[rows[c], :], NT) * weights).astype(BF)
        wq[c] = scores
        attn[rows[c], :] = mm(scores, v[rows[c], :], NN)
    loads[3].wait()
    loads[4].wait()
    loads[5].wait()
    gain = gain_ref[...]
    for c in range(count):
        prob = jax.nn.sigmoid(gi[rows[c], :].astype(F32))
        gate[rows[c], :] = prob
        signal[rows[c], :] = go[rows[c], :].astype(F32) * prob * gain

    acc[...] = jnp.zeros_like(acc)
    for r in range(n_ctx - 1, 0, -1):
        @pl.when(me >= r)
        def _(r=r):
            forward_copy(r).wait_recv()
            acc[...] = jnp.exp(frecv[r, dim : dim + 1, :]) * acc[...] + frecv[r, 0:dim, :]

    state = acc[...]
    ones = jnp.ones((8, dim), BF)
    for c in range(count):
        high, low = split(state)
        ent[c, :, 0:dim] = high
        ent[c, :, dim : 2 * dim] = low
        both = mm(q[rows[c], :], ent[c], NN)
        full = attn[rows[c], :] + fd[rows[c], :] * (both[:, 0:dim] + both[:, dim : 2 * dim])
        attn[rows[c], :] = full
        rsend[0:1, rows[c]] = mm(ones, (full * full).astype(BF), NT)[0:1, :]
        rsend[1:2, rows[c]] = mm(ones, (signal[rows[c], :] * full).astype(BF), NT)[0:1, :]
        if c + 1 < count:
            state = jnp.exp(ends[c]) * state + upd[c]

    for r in range(1, n_norm):
        row_copy(r).start()
    coef[...] = jnp.zeros_like(coef)
    sums = rsend[...]
    for r in range(1, n_norm):
        row_copy(r).wait_recv()
        sums = sums + rrecv[r]
    inv = lax.rsqrt(sums[0:1, :] / width + epsilon)
    coef[0:1, :] = inv
    coef[1:2, :] = inv * inv * (sums[1:2, :] / width)

    seen = [None] * count
    for c in range(count):
        turned = jnp.transpose(coef[:, rows[c]])
        inv_b = jnp.broadcast_to(turned[:, 0:1], (chunk, dim))
        along_b = jnp.broadcast_to(turned[:, 1:2], (chunk, dim))
        full = attn[rows[c], :]
        grad = (inv_b * (signal[rows[c], :] - full * along_b)).astype(BF)
        g[rows[c], :] = grad
        high, low = split(q[rows[c], :].astype(F32) * fd[rows[c], :])
        seen[c] = mm(high, grad, TN) + mm(low, grad, TN)
        upd[c] = seen[c]
        scaled = full * inv_b * gain
        prob = gate[rows[c], :]
        out = scaled * prob
        lo[rows[c], :] = out.astype(BF)
        gg[rows[c], :] = (go[rows[c], :].astype(F32) * out * (1.0 - prob)).astype(BF)
    local = None
    for c in range(count - 1, -1, -1):
        local = seen[c] if local is None else jnp.exp(ends[c]) * local + seen[c]
    bsend[0:dim, :] = local
    bsend[dim : dim + EXTRA, :] = jnp.broadcast_to(total, (EXTRA, dim))
    for r in range(1, n_ctx):
        @pl.when(me >= r)
        def _(r=r):
            backward_copy(r).start()
    stores[0].start()
    stores[1].start()

    for c in range(count):
        grad = g[rows[c], :]
        dv = (mm(grad, v[rows[c], :], NT) * table[c]).astype(BF)
        high = mm(grad, ent[c, :, 0:dim], NT)
        low = mm(grad, ent[c, :, dim : 2 * dim], NT)
        gq[rows[c], :] = (
            mm(dv, k[rows[c], :], NN) + fd[rows[c], :] * (high + low)
        ).astype(BF)
        gkl[rows[c], :] = mm(dv, q[rows[c], :], TN)
        gvl[rows[c], :] = mm(wq[c], grad, TN)
    stores[2].start()

    acc[...] = jnp.zeros_like(acc)
    for r in range(n_ctx - 1, 0, -1):
        @pl.when(me + r < n_ctx)
        def _(r=r):
            backward_copy(r).wait_recv()
            acc[...] = jnp.exp(brecv[r, dim : dim + 1, :]) * acc[...] + brecv[r, 0:dim, :]

    state = acc[...]
    for c in range(count - 1, -1, -1):
        high, low = split(state)
        fall = tail[rows[c], :]
        vc = v[rows[c], :]
        kc = k[rows[c], :]
        gk[rows[c], :] = (gkl[rows[c], :] + fall * (mm(vc, high, NT) + mm(vc, low, NT))).astype(BF)
        gv[rows[c], :] = (gvl[rows[c], :] + fall * (mm(kc, high, NN) + mm(kc, low, NN))).astype(BF)
        if c > 0:
            state = jnp.exp(ends[c]) * state + upd[c]
    stores[3].start()
    stores[4].start()

    for r in range(1, n_ctx):
        @pl.when(me + r < n_ctx)
        def _(r=r):
            forward_copy(r).wait_send()

        @pl.when(me >= r)
        def _(r=r):
            backward_copy(r).wait_send()
    for r in range(1, n_norm):
        row_copy(r).wait_send()
    for copy in stores:
        copy.wait()


def hand_out(*refs):
    copies = [pltpu.make_async_copy(refs[i], refs[5 + i], refs[10].at[i]) for i in range(5)]
    for copy in copies:
        copy.start()
    for copy in copies:
        copy.wait()


def on_device(n_ctx, n_sec, n_exp, queries, key_rows, value_rows, gate_input, norm_gain, log_decay, grad_output):
    length, dim = queries.shape
    assert log_decay.shape[0] == 1
    chunk = min(256, length)
    count = length // chunk
    assert count * chunk == length and count <= 8
    n_norm = n_sec * n_exp
    any_spec = pl.BlockSpec(memory_space=pl.ANY)
    hbm_spec = pl.BlockSpec(memory_space=pltpu.HBM)
    block = lambda dtype: pltpu.VMEM((length, dim), dtype)
    sem = lambda n: pltpu.SemaphoreType.DMA((n,))
    results = pl.pallas_call(
        partial(kernel, (n_ctx, n_sec, n_exp, chunk)),
        out_shape=[jax.ShapeDtypeStruct((length, dim), BF)] * 5,
        in_specs=[hbm_spec] * 7,
        out_specs=[any_spec] * 5,
        scratch_shapes=[block(BF)] * 10
        + [
            pltpu.VMEM((1, dim), F32),
            pltpu.VMEM((1, length), F32),
            pltpu.VMEM((8, chunk), F32),
            block(F32),
            block(F32),
            pltpu.VMEM((count, chunk, chunk), F32),
            pltpu.VMEM((count, chunk, chunk), BF),
            block(F32),
            block(F32),
            block(F32),
            pltpu.VMEM((count, dim, dim), F32),
            pltpu.VMEM((count, dim, 2 * dim), BF),
            block(BF),
            block(F32),
            block(F32),
            pltpu.VMEM((dim + EXTRA, dim), F32),
            pltpu.VMEM((n_ctx, dim + EXTRA, dim), F32),
            pltpu.VMEM((dim + EXTRA, dim), F32),
            pltpu.VMEM((n_ctx, dim + EXTRA, dim), F32),
            pltpu.VMEM((dim, dim), F32),
            pltpu.VMEM((2, length), F32),
            pltpu.VMEM((n_norm, 2, length), F32),
            pltpu.VMEM((8, length), F32),
            sem(7), sem(5), sem(n_ctx), sem(n_ctx), sem(n_ctx), sem(n_ctx), sem(n_norm), sem(n_norm),
        ],
        compiler_params=pltpu.CompilerParams(
            collective_id=0, has_side_effects=True, vmem_limit_bytes=48 * 1024 * 1024
        ),
    )(*[
        pltpu.with_memory_space_constraint(x, pltpu.HBM)
        for x in (queries, key_rows, value_rows, gate_input, grad_output, norm_gain.reshape(1, dim), log_decay)
    ])
    return pl.pallas_call(
        hand_out,
        out_shape=[jax.ShapeDtypeStruct((length, dim), BF)] * 5,
        in_specs=[any_spec] * 5,
        out_specs=[hbm_spec] * 5,
        scratch_shapes=[sem(5)],
        compiler_params=pltpu.CompilerParams(vmem_limit_bytes=2 * 1024 * 1024),
    )(*[pltpu.with_memory_space_constraint(x, pltpu.VMEM) for x in results])


def solution(mesh):
    rows = P("ctx", ("section", "exp"))
    in_specs = (rows, rows, rows, rows, P(("section", "exp")), P(("section", "exp"), "ctx"), rows)
    call = partial(on_device, mesh.shape["ctx"], mesh.shape["section"], mesh.shape["exp"])

    def run(*args):
        return tuple(call(*args))

    return jax.shard_map(run, mesh=mesh, in_specs=in_specs, out_specs=(rows,) * 5, check_vma=False)
```

```python
from functools import partial

import jax
import jax.numpy as jnp
from jax import lax
from jax.experimental import pallas as pl
from jax.experimental.pallas import tpu as pltpu
from jax.sharding import PartitionSpec as P

MESH = pl.DeviceIdType.MESH
BF = jnp.bfloat16
F32 = jnp.float32
epsilon = 1e-06
EXTRA = 8

NN = (((1,), (0,)), ((), ()))
NT = (((1,), (1,)), ((), ()))
TN = (((0,), (0,)), ((), ()))


def mm(a, b, dims):
    return lax.dot_general(a, b, dims, preferred_element_type=F32)


def split(x):
    high = x.astype(BF)
    return high, (x - high.astype(F32)).astype(BF)


def prefix_rows(x):
    lane = lax.broadcasted_iota(jnp.int32, x.shape, 1)
    shift = 1
    while shift < x.shape[1]:
        x = x + jnp.where(lane >= shift, pltpu.roll(x, shift, 1), 0.0)
        shift *= 2
    return x


def kernel(
    sizes,
    q_h, k_h, v_h, gi_h, go_h, gain_h, ld_h,
    lo, gq, gk, gv, gg,
    q, k, v, gi, go,
    gain_ref, ld_ref, steps, fd, tail, table, wq, attn, signal, gate, upd, ent, g, gkl, gvl, turned_q, inv_cols,
    fsend, frecv, bsend, brecv, acc, rsend, rrecv, coef,
    in_sem, fs_sem, fr_sem, bs_sem, br_sem, rs_sem, rr_sem,
):
    n_ctx, n_sec, n_exp, chunk = sizes
    n_norm = n_sec * n_exp
    length, dim = q.shape
    count = length // chunk
    me = lax.axis_index("ctx")
    pair = 2 if n_ctx % 2 == 0 else 1
    n_row = n_ctx // pair
    row, core = lax.div(me, pair), lax.rem(me, pair)
    sec = lax.axis_index("section")
    ex = lax.axis_index("exp")
    mine = sec * n_exp + ex
    width = float(dim * n_norm)

    def norm_peer(r):
        other = lax.rem(mine + r, n_norm)
        return {"section": lax.div(other, n_exp), "exp": lax.rem(other, n_exp)}

    loads = [
        pltpu.make_async_copy(src, dst, in_sem.at[i])
        for i, (src, dst) in enumerate(
            ((k_h, k), (v_h, v), (q_h, q), (gi_h, gi), (go_h, go), (gain_h, gain_ref), (ld_h, ld_ref))
        )
    ]
    for i in (6, 0, 1, 2, 3, 4, 5):
        loads[i].start()

    barrier = pltpu.get_barrier_semaphore()
    for r in range(1, n_row):
        other = lax.rem(row + r, n_row) * pair + core
        pl.semaphore_signal(barrier, inc=1, device_id={"ctx": other}, device_id_type=MESH)
    if pair == 2:
        twin = row * pair + 1 - core
        pl.semaphore_signal(barrier, inc=1, device_id={"ctx": twin}, device_id_type=MESH)
    for r in range(1, n_norm):
        pl.semaphore_signal(barrier, inc=1, device_id=norm_peer(r), device_id_type=MESH)

    rows = [pl.ds(c * chunk, chunk) for c in range(count)]

    steps[...] = jnp.zeros_like(steps)
    loads[6].wait()
    for c in range(count):
        steps[c : c + 1, :] = ld_ref[:, c * chunk : (c + 1) * chunk]
    run = prefix_rows(steps[...])
    steps[...] = run
    run_t = jnp.transpose(run)
    ends = [run[c : c + 1, chunk - 1 : chunk] for c in range(count)]
    for c in range(count):
        column = jnp.broadcast_to(run_t[:, c : c + 1], (chunk, dim))
        fd[rows[c], :] = jnp.exp(column)
        tail[rows[c], :] = jnp.exp(ends[c] - column)

    loads[0].wait()
    loads[1].wait()
    local = None
    total = None
    for c in range(count):
        high, low = split(k[rows[c], :].astype(F32) * tail[rows[c], :])
        vc = v[rows[c], :]
        update = mm(high, vc, TN) + mm(low, vc, TN)
        upd[c] = update
        local = update if local is None else jnp.exp(ends[c]) * local + update
        total = ends[c] if total is None else total + ends[c]
    fsend[0:dim, :] = local
    fsend[dim : dim + EXTRA, :] = jnp.broadcast_to(total, (EXTRA, dim))

    pl.semaphore_wait(barrier, n_row - 1 + pair - 1 + n_norm - 1)

    def exchange(reverse, send, recv, s_sem, r_sem):
        y, c = (n_row - 1 - row, pair - 1 - core) if reverse else (row, core)

        def to(y_to, c_to):
            if reverse:
                y_to, c_to = n_row - 1 - y_to, pair - 1 - c_to
            return {"ctx": y_to * pair + c_to}

        def copy(src, slot, target):
            return pltpu.make_async_remote_copy(
                src_ref=src, dst_ref=recv.at[slot], send_sem=s_sem.at[slot],
                recv_sem=r_sem.at[slot], device_id=target, device_id_type=MESH,
            )

        def direct(d):
            return copy(send, d * pair, to(lax.rem(y + d, n_row), c))

        def relay(d):
            return copy(recv.at[d * pair], d * pair + 1, to(y, 1 - c))

        def neighbour():
            return copy(send, 1, to(y, 1 - c))

        def start():
            for d in range(1, n_row):
                @pl.when(y + d < n_row)
                def _(d=d):
                    direct(d).start()
            if pair == 2:
                @pl.when(c == 0)
                def _():
                    neighbour().start()

        def pass_on():
            for d in range(1, n_row):
                @pl.when(y >= d)
                def _(d=d):
                    direct(d).wait_recv()
                    if pair == 2:
                        relay(d).start()

        def join(slot):
            acc[...] = jnp.exp(recv[slot, dim : dim + 1, :]) * acc[...] + recv[slot, 0:dim, :]

        def collect():
            acc[...] = jnp.zeros_like(acc)
            for d in range(n_row - 1, 0, -1):
                @pl.when(y >= d)
                def _(d=d):
                    if pair == 2:
                        relay(d).wait_recv()
                        join(d * pair + c)
                        join(d * pair + 1 - c)
                    else:
                        join(d)
            if pair == 2:
                @pl.when(c == 1)
                def _():
                    neighbour().wait_recv()
                    join(1)

        def finish():
            for d in range(1, n_row):
                @pl.when(y + d < n_row)
                def _(d=d):
                    direct(d).wait_send()
                if pair == 2:
                    @pl.when(y >= d)
                    def _(d=d):
                        relay(d).wait_send()
            if pair == 2:
                @pl.when(c == 0)
                def _():
                    neighbour().wait_send()

        return start, pass_on, collect, finish

    forward = exchange(False, fsend, frecv, fs_sem, fr_sem)
    backward = exchange(True, bsend, brecv, bs_sem, br_sem)

    def row_copy(r):
        return pltpu.make_async_remote_copy(
            src_ref=rsend, dst_ref=rrecv.at[r], send_sem=rs_sem.at[r], recv_sem=rr_sem.at[r],
            device_id=norm_peer(r), device_id_type=MESH,
        )

    forward[0]()

    loads[2].wait()
    t_index = lax.broadcasted_iota(jnp.int32, (chunk, chunk), 0)
    s_index = lax.broadcasted_iota(jnp.int32, (chunk, chunk), 1)
    for c in range(count):
        column = jnp.broadcast_to(run_t[:, c : c + 1], (chunk, chunk))
        gap = jnp.minimum(column - steps[c : c + 1, :], 0.0)
        weights = jnp.where(t_index >= s_index, jnp.exp(gap), 0.0)
        table[c] = weights
        scores = (mm(q[rows[c], :], k[rows[c], :], NT) * weights).astype(BF)
        wq[c] = scores
        attn[rows[c], :] = mm(scores, v[rows[c], :], NN)
    forward[1]()
    loads[3].wait()
    loads[4].wait()
    loads[5].wait()
    gain = gain_ref[...]
    for c in range(count):
        prob = jax.nn.sigmoid(gi[rows[c], :].astype(F32))
        gate[rows[c], :] = prob
        signal[rows[c], :] = go[rows[c], :].astype(F32) * prob * gain

    forward[2]()

    state = acc[...]
    ones = jnp.ones((8, dim), BF)
    for c in range(count):
        high, low = split(state)
        ent[c, :, 0:dim] = high
        ent[c, :, dim : 2 * dim] = low
        both = mm(q[rows[c], :], ent[c], NN)
        full = attn[rows[c], :] + fd[rows[c], :] * (both[:, 0:dim] + both[:, dim : 2 * dim])
        attn[rows[c], :] = full
        rsend[0:1, rows[c]] = mm(ones, (full * full).astype(BF), NT)[0:1, :]
        rsend[1:2, rows[c]] = mm(ones, (signal[rows[c], :] * full).astype(BF), NT)[0:1, :]
        if c + 1 < count:
            state = jnp.exp(ends[c]) * state + upd[c]

    for r in range(1, n_norm):
        row_copy(r).start()
    coef[...] = jnp.zeros_like(coef)
    for c in range(count):
        high, low = split(jnp.transpose(q[rows[c], :].astype(F32) * fd[rows[c], :]))
        turned_q[c, 0:dim, :] = high
        turned_q[c, dim : 2 * dim, :] = low
    sums = rsend[...]
    for r in range(1, n_norm):
        row_copy(r).wait_recv()
        sums = sums + rrecv[r]
    inv = lax.rsqrt(sums[0:1, :] / width + epsilon)
    coef[0:1, :] = inv
    coef[1:2, :] = inv * inv * (sums[1:2, :] / width)

    seen = [None] * count
    for c in range(count):
        turned = jnp.transpose(coef[:, rows[c]])
        inv_b = jnp.broadcast_to(turned[:, 0:1], (chunk, dim))
        along_b = jnp.broadcast_to(turned[:, 1:2], (chunk, dim))
        full = attn[rows[c], :]
        grad = (inv_b * (signal[rows[c], :] - full * along_b)).astype(BF)
        g[rows[c], :] = grad
        inv_cols[rows[c], :] = inv_b
        both = mm(turned_q[c], grad, NN)
        seen[c] = both[0:dim, :] + both[dim : 2 * dim, :]
        upd[c] = seen[c]
    local = None
    for c in range(count - 1, -1, -1):
        local = seen[c] if local is None else jnp.exp(ends[c]) * local + seen[c]
    bsend[0:dim, :] = local
    bsend[dim : dim + EXTRA, :] = jnp.broadcast_to(total, (EXTRA, dim))
    backward[0]()

    for c in range(count):
        grad = g[rows[c], :]
        dv = (mm(grad, v[rows[c], :], NT) * table[c]).astype(BF)
        high = mm(grad, ent[c, :, 0:dim], NT)
        low = mm(grad, ent[c, :, dim : 2 * dim], NT)
        gq[rows[c], :] = (
            mm(dv, k[rows[c], :], NN) + fd[rows[c], :] * (high + low)
        ).astype(BF)
        gkl[rows[c], :] = mm(dv, q[rows[c], :], TN)
        gvl[rows[c], :] = mm(wq[c], grad, TN)
    backward[1]()
    for c in range(count):
        prob = gate[rows[c], :]
        out = attn[rows[c], :] * inv_cols[rows[c], :] * gain * prob
        lo[rows[c], :] = out.astype(BF)
        gg[rows[c], :] = (go[rows[c], :].astype(F32) * out * (1.0 - prob)).astype(BF)

    backward[2]()

    state = acc[...]
    for c in range(count - 1, -1, -1):
        high, low = split(state)
        fall = tail[rows[c], :]
        vc = v[rows[c], :]
        kc = k[rows[c], :]
        gk[rows[c], :] = (gkl[rows[c], :] + fall * (mm(vc, high, NT) + mm(vc, low, NT))).astype(BF)
        gv[rows[c], :] = (gvl[rows[c], :] + fall * (mm(kc, high, NN) + mm(kc, low, NN))).astype(BF)
        if c > 0:
            state = jnp.exp(ends[c]) * state + upd[c]

    forward[3]()
    backward[3]()
    for r in range(1, n_norm):
        row_copy(r).wait_send()


def hand_out(*refs):
    copies = [pltpu.make_async_copy(refs[i], refs[5 + i], refs[10].at[i]) for i in range(5)]
    for copy in copies:
        copy.start()
    for copy in copies:
        copy.wait()


def on_device(n_ctx, n_sec, n_exp, queries, key_rows, value_rows, gate_input, norm_gain, log_decay, grad_output):
    length, dim = queries.shape
    assert log_decay.shape[0] == 1
    chunk = min(256, length)
    count = length // chunk
    assert count * chunk == length and count <= 8
    n_norm = n_sec * n_exp
    any_spec = pl.BlockSpec(memory_space=pl.ANY)
    hbm_spec = pl.BlockSpec(memory_space=pltpu.HBM)
    block = lambda dtype: pltpu.VMEM((length, dim), dtype)
    sem = lambda n: pltpu.SemaphoreType.DMA((n,))
    results = pl.pallas_call(
        partial(kernel, (n_ctx, n_sec, n_exp, chunk)),
        out_shape=[pltpu.VMEM((length, dim), BF)] * 5,
        in_specs=[hbm_spec] * 7,
        out_specs=[pl.BlockSpec(memory_space=pltpu.VMEM)] * 5,
        scratch_shapes=[block(BF)] * 5
        + [
            pltpu.VMEM((1, dim), F32),
            pltpu.VMEM((1, length), F32),
            pltpu.VMEM((8, chunk), F32),
            block(F32),
            block(F32),
            pltpu.VMEM((count, chunk, chunk), F32),
            pltpu.VMEM((count, chunk, chunk), BF),
            block(F32),
            block(F32),
            block(F32),
            pltpu.VMEM((count, dim, dim), F32),
            pltpu.VMEM((count, dim, 2 * dim), BF),
            block(BF),
            block(F32),
            block(F32),
            pltpu.VMEM((count, 2 * dim, chunk), BF),
            block(F32),
            pltpu.VMEM((dim + EXTRA, dim), F32),
            pltpu.VMEM((n_ctx, dim + EXTRA, dim), F32),
            pltpu.VMEM((dim + EXTRA, dim), F32),
            pltpu.VMEM((n_ctx, dim + EXTRA, dim), F32),
            pltpu.VMEM((dim, dim), F32),
            pltpu.VMEM((2, length), F32),
            pltpu.VMEM((n_norm, 2, length), F32),
            pltpu.VMEM((8, length), F32),
            sem(7), sem(n_ctx), sem(n_ctx), sem(n_ctx), sem(n_ctx), sem(n_norm), sem(n_norm),
        ],
        compiler_params=pltpu.CompilerParams(
            collective_id=0, has_side_effects=True, vmem_limit_bytes=48 * 1024 * 1024
        ),
    )(*[
        pltpu.with_memory_space_constraint(x, pltpu.HBM)
        for x in (queries, key_rows, value_rows, gate_input, grad_output, norm_gain.reshape(1, dim), log_decay)
    ])
    return pl.pallas_call(
        hand_out,
        out_shape=[jax.ShapeDtypeStruct((length, dim), BF)] * 5,
        in_specs=[any_spec] * 5,
        out_specs=[hbm_spec] * 5,
        scratch_shapes=[sem(5)],
        compiler_params=pltpu.CompilerParams(vmem_limit_bytes=2 * 1024 * 1024),
    )(*[pltpu.with_memory_space_constraint(x, pltpu.VMEM) for x in results])


def solution(mesh):
    rows = P("ctx", ("section", "exp"))
    in_specs = (rows, rows, rows, rows, P(("section", "exp")), P(("section", "exp"), "ctx"), rows)
    call = partial(on_device, mesh.shape["ctx"], mesh.shape["section"], mesh.shape["exp"])

    def run(*args):
        return tuple(call(*args))

    return jax.shard_map(run, mesh=mesh, in_specs=in_specs, out_specs=(rows,) * 5, check_vma=False)
```

```python
from functools import partial

import jax
import jax.numpy as jnp
from jax import lax
from jax.experimental import pallas as pl
from jax.experimental.pallas import tpu as pltpu
from jax.sharding import PartitionSpec as P

MESH = pl.DeviceIdType.MESH
BF = jnp.bfloat16
F32 = jnp.float32
epsilon = 1e-06
EXTRA = 8

NN = (((1,), (0,)), ((), ()))
NT = (((1,), (1,)), ((), ()))
TN = (((0,), (0,)), ((), ()))


def mm(a, b, dims):
    return lax.dot_general(a, b, dims, preferred_element_type=F32)


def split(x):
    high = x.astype(BF)
    return high, (x - high.astype(F32)).astype(BF)


def prefix_rows(x):
    lane = lax.broadcasted_iota(jnp.int32, x.shape, 1)
    shift = 1
    while shift < x.shape[1]:
        x = x + jnp.where(lane >= shift, pltpu.roll(x, shift, 1), 0.0)
        shift *= 2
    return x


def kernel(
    sizes,
    q_h, k_h, v_h, gi_h, go_h, gain_h, ld_h,
    lo, gq, gk, gv, gg,
    q, k, v, gi, go,
    gain_ref, ld_ref, steps, fd, tail, table, wq, attn, signal, gate, upd, ent, g, gkl, gvl, turned_q, inv_cols, cols, fall,
    fsend, frecv, bsend, brecv, acc, rsend, rrecv, coef,
    in_sem, fs_sem, fr_sem, bs_sem, br_sem, rs_sem, rr_sem,
):
    n_ctx, n_sec, n_exp, chunk = sizes
    n_norm = n_sec * n_exp
    length, dim = q.shape
    count = length // chunk
    me = lax.axis_index("ctx")
    pair = 2 if n_ctx % 2 == 0 else 1
    n_row = n_ctx // pair
    row, core = lax.div(me, pair), lax.rem(me, pair)
    sec = lax.axis_index("section")
    ex = lax.axis_index("exp")
    mine = sec * n_exp + ex
    width = float(dim * n_norm)

    def norm_peer(r):
        other = lax.rem(mine + r, n_norm)
        return {"section": lax.div(other, n_exp), "exp": lax.rem(other, n_exp)}

    loads = [
        pltpu.make_async_copy(src, dst, in_sem.at[i])
        for i, (src, dst) in enumerate(
            ((k_h, k), (v_h, v), (q_h, q), (gi_h, gi), (go_h, go), (gain_h, gain_ref), (ld_h, ld_ref))
        )
    ]
    for i in (6, 0, 1, 2, 3, 4, 5):
        loads[i].start()

    barrier = pltpu.get_barrier_semaphore()
    for r in range(1, n_row):
        other = lax.rem(row + r, n_row) * pair + core
        pl.semaphore_signal(barrier, inc=1, device_id={"ctx": other}, device_id_type=MESH)
    if pair == 2:
        twin = row * pair + 1 - core
        pl.semaphore_signal(barrier, inc=1, device_id={"ctx": twin}, device_id_type=MESH)
    for r in range(1, n_norm):
        pl.semaphore_signal(barrier, inc=1, device_id=norm_peer(r), device_id_type=MESH)

    rows = [pl.ds(c * chunk, chunk) for c in range(count)]

    steps[...] = jnp.zeros_like(steps)
    loads[6].wait()
    for c in range(count):
        steps[c : c + 1, :] = ld_ref[:, c * chunk : (c + 1) * chunk]
    run = prefix_rows(steps[...])
    steps[...] = run
    run_t = jnp.transpose(run)
    ends = [run[c : c + 1, chunk - 1 : chunk] for c in range(count)]
    for c in range(count):
        column = jnp.broadcast_to(run_t[:, c : c + 1], (chunk, dim))
        cols[rows[c], :] = column
        tail[rows[c], :] = jnp.exp(ends[c] - column)
        fall[c : c + 1, :] = jnp.broadcast_to(jnp.exp(ends[c]), (1, dim))

    def each(body):
        def one(c, carry):
            body(c, pl.ds(pl.multiple_of(c * chunk, chunk), chunk))
            return carry

        lax.fori_loop(0, count, one, 0)

    loads[0].wait()
    loads[1].wait()
    local = None
    total = None
    for c in range(count):
        high, low = split(k[rows[c], :].astype(F32) * tail[rows[c], :])
        vc = v[rows[c], :]
        update = mm(high, vc, TN) + mm(low, vc, TN)
        upd[c] = update
        local = update if local is None else jnp.exp(ends[c]) * local + update
        total = ends[c] if total is None else total + ends[c]
    fsend[0:dim, :] = local
    fsend[dim : dim + EXTRA, :] = jnp.broadcast_to(total, (EXTRA, dim))

    pl.semaphore_wait(barrier, n_row - 1 + pair - 1 + n_norm - 1)

    def exchange(reverse, send, recv, s_sem, r_sem):
        y, c = (n_row - 1 - row, pair - 1 - core) if reverse else (row, core)

        def to(y_to, c_to):
            if reverse:
                y_to, c_to = n_row - 1 - y_to, pair - 1 - c_to
            return {"ctx": y_to * pair + c_to}

        def copy(src, slot, target):
            return pltpu.make_async_remote_copy(
                src_ref=src, dst_ref=recv.at[slot], send_sem=s_sem.at[slot],
                recv_sem=r_sem.at[slot], device_id=target, device_id_type=MESH,
            )

        def direct(d):
            return copy(send, d * pair, to(lax.rem(y + d, n_row), c))

        def relay(d):
            return copy(recv.at[d * pair], d * pair + 1, to(y, 1 - c))

        def neighbour():
            return copy(send, 1, to(y, 1 - c))

        def start():
            for d in range(1, n_row):
                @pl.when(y + d < n_row)
                def _(d=d):
                    direct(d).start()
            if pair == 2:
                @pl.when(c == 0)
                def _():
                    neighbour().start()

        def pass_on():
            for d in range(1, n_row):
                @pl.when(y >= d)
                def _(d=d):
                    direct(d).wait_recv()
                    if pair == 2:
                        relay(d).start()

        def join(slot):
            acc[...] = jnp.exp(recv[slot, dim : dim + 1, :]) * acc[...] + recv[slot, 0:dim, :]

        def collect():
            acc[...] = jnp.zeros_like(acc)
            for d in range(n_row - 1, 0, -1):
                @pl.when(y >= d)
                def _(d=d):
                    if pair == 2:
                        relay(d).wait_recv()
                        join(d * pair + c)
                        join(d * pair + 1 - c)
                    else:
                        join(d)
            if pair == 2:
                @pl.when(c == 1)
                def _():
                    neighbour().wait_recv()
                    join(1)

        def finish():
            for d in range(1, n_row):
                @pl.when(y + d < n_row)
                def _(d=d):
                    direct(d).wait_send()
                if pair == 2:
                    @pl.when(y >= d)
                    def _(d=d):
                        relay(d).wait_send()
            if pair == 2:
                @pl.when(c == 0)
                def _():
                    neighbour().wait_send()

        return start, pass_on, collect, finish

    forward = exchange(False, fsend, frecv, fs_sem, fr_sem)
    backward = exchange(True, bsend, brecv, bs_sem, br_sem)

    def row_copy(r):
        return pltpu.make_async_remote_copy(
            src_ref=rsend, dst_ref=rrecv.at[r], send_sem=rs_sem.at[r], recv_sem=rr_sem.at[r],
            device_id=norm_peer(r), device_id_type=MESH,
        )

    forward[0]()

    loads[2].wait()
    t_index = lax.broadcasted_iota(jnp.int32, (chunk, chunk), 0)
    s_index = lax.broadcasted_iota(jnp.int32, (chunk, chunk), 1)

    def inside(c, here):
        column = cols[here, :]
        fd[here, :] = jnp.exp(column)
        column = jnp.concatenate([column] * (chunk // dim), axis=1) if chunk >= dim else column[:, :chunk]
        gap = jnp.minimum(column - steps[pl.ds(c, 1), :], 0.0)
        weights = jnp.where(t_index >= s_index, jnp.exp(gap), 0.0)
        table[c] = weights
        scores = (mm(q[here, :], k[here, :], NT) * weights).astype(BF)
        wq[c] = scores
        attn[here, :] = mm(scores, v[here, :], NN)

    each(inside)
    forward[1]()
    loads[3].wait()
    loads[4].wait()
    loads[5].wait()
    gain = gain_ref[...]

    def gating(c, here):
        prob = jax.nn.sigmoid(gi[here, :].astype(F32))
        gate[here, :] = prob
        signal[here, :] = go[here, :].astype(F32) * prob * gain

    each(gating)

    forward[2]()

    ones = jnp.ones((8, dim), BF)

    def attending(c, here):
        state = acc[...]
        high, low = split(state)
        both = mm(q[here, :], jnp.concatenate([high, low], axis=1), NN)
        ent[c, :, 0:dim] = high
        ent[c, :, dim : 2 * dim] = low
        full = attn[here, :] + fd[here, :] * (both[:, 0:dim] + both[:, dim : 2 * dim])
        attn[here, :] = full
        rsend[0:1, here] = mm(ones, (full * full).astype(BF), NT)[0:1, :]
        rsend[1:2, here] = mm(ones, (signal[here, :] * full).astype(BF), NT)[0:1, :]
        acc[...] = fall[pl.ds(c, 1), :] * state + upd[c]

    each(attending)
    for r in range(1, n_norm):
        row_copy(r).start()
    coef[...] = jnp.zeros_like(coef)

    def turning(c, here):
        high, low = split(jnp.transpose(q[here, :].astype(F32) * fd[here, :]))
        turned_q[c, 0:dim, :] = high
        turned_q[c, dim : 2 * dim, :] = low

    each(turning)
    sums = rsend[...]
    for r in range(1, n_norm):
        row_copy(r).wait_recv()
        sums = sums + rrecv[r]
    inv = lax.rsqrt(sums[0:1, :] / width + epsilon)
    coef[0:1, :] = inv
    coef[1:2, :] = inv * inv * (sums[1:2, :] / width)

    bsend[0:dim, :] = jnp.zeros((dim, dim), F32)

    def grading(turn, carry):
        c = count - 1 - turn
        here = pl.ds(pl.multiple_of(c * chunk, chunk), chunk)
        turned = jnp.transpose(coef[:, here])
        inv_b = jnp.broadcast_to(turned[:, 0:1], (chunk, dim))
        along_b = jnp.broadcast_to(turned[:, 1:2], (chunk, dim))
        grad = (inv_b * (signal[here, :] - attn[here, :] * along_b)).astype(BF)
        g[here, :] = grad
        inv_cols[here, :] = inv_b
        both = mm(turned_q[c], grad, NN)
        seen = both[0:dim, :] + both[dim : 2 * dim, :]
        upd[c] = seen
        bsend[0:dim, :] = fall[pl.ds(c, 1), :] * bsend[0:dim, :] + seen
        return carry

    lax.fori_loop(0, count, grading, 0)
    bsend[dim : dim + EXTRA, :] = jnp.broadcast_to(total, (EXTRA, dim))
    backward[0]()

    def products(c, here):
        grad = g[here, :]
        dv = (mm(grad, v[here, :], NT) * table[c]).astype(BF)
        high = mm(grad, ent[c, :, 0:dim], NT)
        low = mm(grad, ent[c, :, dim : 2 * dim], NT)
        gq[here, :] = (mm(dv, k[here, :], NN) + fd[here, :] * (high + low)).astype(BF)
        gkl[here, :] = mm(dv, q[here, :], TN)
        gvl[here, :] = mm(wq[c], grad, TN)

    each(products)
    backward[1]()

    def gated(c, here):
        prob = gate[here, :]
        out = attn[here, :] * inv_cols[here, :] * gain * prob
        lo[here, :] = out.astype(BF)
        gg[here, :] = (go[here, :].astype(F32) * out * (1.0 - prob)).astype(BF)

    each(gated)

    backward[2]()

    def finishing(turn, carry):
        c = count - 1 - turn
        here = pl.ds(pl.multiple_of(c * chunk, chunk), chunk)
        state = acc[...]
        high, low = split(state)
        left = tail[here, :]
        vc = v[here, :]
        kc = k[here, :]
        gk[here, :] = (gkl[here, :] + left * (mm(vc, high, NT) + mm(vc, low, NT))).astype(BF)
        gv[here, :] = (gvl[here, :] + left * (mm(kc, high, NN) + mm(kc, low, NN))).astype(BF)
        acc[...] = fall[pl.ds(c, 1), :] * state + upd[c]
        return carry

    lax.fori_loop(0, count, finishing, 0)

    forward[3]()
    backward[3]()
    for r in range(1, n_norm):
        row_copy(r).wait_send()


def hand_out(*refs):
    copies = [pltpu.make_async_copy(refs[i], refs[5 + i], refs[10].at[i]) for i in range(5)]
    for copy in copies:
        copy.start()
    for copy in copies:
        copy.wait()


def on_device(n_ctx, n_sec, n_exp, queries, key_rows, value_rows, gate_input, norm_gain, log_decay, grad_output):
    length, dim = queries.shape
    assert log_decay.shape[0] == 1
    chunk = min(256, length)
    count = length // chunk
    assert count * chunk == length and count <= 8
    n_norm = n_sec * n_exp
    any_spec = pl.BlockSpec(memory_space=pl.ANY)
    hbm_spec = pl.BlockSpec(memory_space=pltpu.HBM)
    block = lambda dtype: pltpu.VMEM((length, dim), dtype)
    sem = lambda n: pltpu.SemaphoreType.DMA((n,))
    results = pl.pallas_call(
        partial(kernel, (n_ctx, n_sec, n_exp, chunk)),
        out_shape=[pltpu.VMEM((length, dim), BF)] * 5,
        in_specs=[hbm_spec] * 7,
        out_specs=[pl.BlockSpec(memory_space=pltpu.VMEM)] * 5,
        scratch_shapes=[block(BF)] * 5
        + [
            pltpu.VMEM((1, dim), F32),
            pltpu.VMEM((1, length), F32),
            pltpu.VMEM((8, chunk), F32),
            block(F32),
            block(F32),
            pltpu.VMEM((count, chunk, chunk), F32),
            pltpu.VMEM((count, chunk, chunk), BF),
            block(F32),
            block(F32),
            block(F32),
            pltpu.VMEM((count, dim, dim), F32),
            pltpu.VMEM((count, dim, 2 * dim), BF),
            block(BF),
            block(F32),
            block(F32),
            pltpu.VMEM((count, 2 * dim, chunk), BF),
            block(F32),
            block(F32),
            pltpu.VMEM((8, dim), F32),
            pltpu.VMEM((dim + EXTRA, dim), F32),
            pltpu.VMEM((n_ctx, dim + EXTRA, dim), F32),
            pltpu.VMEM((dim + EXTRA, dim), F32),
            pltpu.VMEM((n_ctx, dim + EXTRA, dim), F32),
            pltpu.VMEM((dim, dim), F32),
            pltpu.VMEM((2, length), F32),
            pltpu.VMEM((n_norm, 2, length), F32),
            pltpu.VMEM((8, length), F32),
            sem(7), sem(n_ctx), sem(n_ctx), sem(n_ctx), sem(n_ctx), sem(n_norm), sem(n_norm),
        ],
        compiler_params=pltpu.CompilerParams(
            collective_id=0, has_side_effects=True, vmem_limit_bytes=48 * 1024 * 1024
        ),
    )(*[
        pltpu.with_memory_space_constraint(x, pltpu.HBM)
        for x in (queries, key_rows, value_rows, gate_input, grad_output, norm_gain.reshape(1, dim), log_decay)
    ])
    return pl.pallas_call(
        hand_out,
        out_shape=[jax.ShapeDtypeStruct((length, dim), BF)] * 5,
        in_specs=[any_spec] * 5,
        out_specs=[hbm_spec] * 5,
        scratch_shapes=[sem(5)],
        compiler_params=pltpu.CompilerParams(vmem_limit_bytes=2 * 1024 * 1024),
    )(*[pltpu.with_memory_space_constraint(x, pltpu.VMEM) for x in results])


def solution(mesh):
    rows = P("ctx", ("section", "exp"))
    in_specs = (rows, rows, rows, rows, P(("section", "exp")), P(("section", "exp"), "ctx"), rows)
    call = partial(on_device, mesh.shape["ctx"], mesh.shape["section"], mesh.shape["exp"])

    def run(*args):
        return tuple(call(*args))

    return jax.shard_map(run, mesh=mesh, in_specs=in_specs, out_specs=(rows,) * 5, check_vma=False)
```

```python
from functools import partial

import jax
import jax.numpy as jnp
from jax import lax
from jax.experimental import pallas as pl
from jax.experimental.pallas import tpu as pltpu
from jax.sharding import PartitionSpec as P

MESH = pl.DeviceIdType.MESH
BF = jnp.bfloat16
F32 = jnp.float32
epsilon = 1e-06
EXTRA = 8

NN = (((1,), (0,)), ((), ()))
NT = (((1,), (1,)), ((), ()))
TN = (((0,), (0,)), ((), ()))


def mm(a, b, dims):
    return lax.dot_general(a, b, dims, preferred_element_type=F32)


def split(x):
    high = x.astype(BF)
    return high, (x - high.astype(F32)).astype(BF)


def prefix_rows(x):
    size = x.shape[1]
    first = lax.broadcasted_iota(jnp.int32, (size, size), 0)
    last = lax.broadcasted_iota(jnp.int32, (size, size), 1)
    upto = jnp.where(first <= last, 1.0, 0.0).astype(BF)
    high, low = split(x)
    rest = (x - high.astype(F32) - low.astype(F32)).astype(BF)
    return mm(high, upto, NN) + (mm(low, upto, NN) + mm(rest, upto, NN))


def kernel(
    sizes,
    q_h, k_h, v_h, gi_h, go_h, gain_h, ld_h,
    lo, gq, gk, gv, gg,
    q, k, v, gi, go,
    gain_ref, ld_ref, steps, fd, tail, table, wq, attn, signal, gate, upd, ent, g, gkl, gvl, turned_q, inv_cols,
    fsend, frecv, bsend, brecv, acc, rsend, rrecv, coef,
    in_sem, fs_sem, fr_sem, bs_sem, br_sem, rs_sem, rr_sem,
):
    n_ctx, n_sec, n_exp, chunk = sizes
    n_norm = n_sec * n_exp
    length, dim = q.shape
    count = length // chunk
    me = lax.axis_index("ctx")
    pair = 2 if n_ctx % 2 == 0 else 1
    n_row = n_ctx // pair
    row, core = lax.div(me, pair), lax.rem(me, pair)
    sec = lax.axis_index("section")
    ex = lax.axis_index("exp")
    mine = sec * n_exp + ex
    width = float(dim * n_norm)

    def norm_peer(r):
        other = lax.rem(mine + r, n_norm)
        return {"section": lax.div(other, n_exp), "exp": lax.rem(other, n_exp)}

    loads = [
        pltpu.make_async_copy(src, dst, in_sem.at[i])
        for i, (src, dst) in enumerate(
            ((k_h, k), (v_h, v), (q_h, q), (gi_h, gi), (go_h, go), (gain_h, gain_ref), (ld_h, ld_ref))
        )
    ]
    for i in (6, 0, 1, 2, 3, 4, 5):
        loads[i].start()

    barrier = pltpu.get_barrier_semaphore()
    for r in range(1, n_row):
        other = lax.rem(row + r, n_row) * pair + core
        pl.semaphore_signal(barrier, inc=1, device_id={"ctx": other}, device_id_type=MESH)
    if pair == 2:
        twin = row * pair + 1 - core
        pl.semaphore_signal(barrier, inc=1, device_id={"ctx": twin}, device_id_type=MESH)
    for r in range(1, n_norm):
        pl.semaphore_signal(barrier, inc=1, device_id=norm_peer(r), device_id_type=MESH)

    rows = [pl.ds(c * chunk, chunk) for c in range(count)]

    steps[...] = jnp.zeros_like(steps)
    loads[6].wait()
    for c in range(count):
        steps[c : c + 1, :] = ld_ref[:, c * chunk : (c + 1) * chunk]
    run = prefix_rows(steps[...])
    steps[...] = run
    run_t = jnp.transpose(run)
    ends = [run[c : c + 1, chunk - 1 : chunk] for c in range(count)]
    for c in range(count):
        column = jnp.broadcast_to(run_t[:, c : c + 1], (chunk, dim))
        tail[rows[c], :] = jnp.exp(ends[c] - column)

    loads[0].wait()
    loads[1].wait()
    local = None
    total = None
    for c in range(count):
        high, low = split(k[rows[c], :].astype(F32) * tail[rows[c], :])
        vc = v[rows[c], :]
        update = mm(high, vc, TN) + mm(low, vc, TN)
        upd[c] = update
        local = update if local is None else jnp.exp(ends[c]) * local + update
        total = ends[c] if total is None else total + ends[c]
    fsend[0:dim, :] = local
    fsend[dim : dim + EXTRA, :] = jnp.broadcast_to(total, (EXTRA, dim))

    pl.semaphore_wait(barrier, n_row - 1 + pair - 1 + n_norm - 1)

    def exchange(reverse, send, recv, s_sem, r_sem):
        y, c = (n_row - 1 - row, pair - 1 - core) if reverse else (row, core)

        def to(y_to, c_to):
            if reverse:
                y_to, c_to = n_row - 1 - y_to, pair - 1 - c_to
            return {"ctx": y_to * pair + c_to}

        def copy(src, slot, target):
            return pltpu.make_async_remote_copy(
                src_ref=src, dst_ref=recv.at[slot], send_sem=s_sem.at[slot],
                recv_sem=r_sem.at[slot], device_id=target, device_id_type=MESH,
            )

        def direct(d):
            return copy(send, d * pair, to(lax.rem(y + d, n_row), c))

        def relay(d):
            return copy(recv.at[d * pair], d * pair + 1, to(y, 1 - c))

        def neighbour():
            return copy(send, 1, to(y, 1 - c))

        def start():
            for d in range(1, n_row):
                @pl.when(y + d < n_row)
                def _(d=d):
                    direct(d).start()
            if pair == 2:
                @pl.when(c == 0)
                def _():
                    neighbour().start()

        def pass_on():
            for d in range(1, n_row):
                @pl.when(y >= d)
                def _(d=d):
                    direct(d).wait_recv()
                    if pair == 2:
                        relay(d).start()

        def join(slot):
            acc[...] = jnp.exp(recv[slot, dim : dim + 1, :]) * acc[...] + recv[slot, 0:dim, :]

        def collect():
            acc[...] = jnp.zeros_like(acc)
            for d in range(n_row - 1, 0, -1):
                @pl.when(y >= d)
                def _(d=d):
                    if pair == 2:
                        relay(d).wait_recv()
                        join(d * pair + c)
                        join(d * pair + 1 - c)
                    else:
                        join(d)
            if pair == 2:
                @pl.when(c == 1)
                def _():
                    neighbour().wait_recv()
                    join(1)

        def finish():
            for d in range(1, n_row):
                @pl.when(y + d < n_row)
                def _(d=d):
                    direct(d).wait_send()
                if pair == 2:
                    @pl.when(y >= d)
                    def _(d=d):
                        relay(d).wait_send()
            if pair == 2:
                @pl.when(c == 0)
                def _():
                    neighbour().wait_send()

        return start, pass_on, collect, finish

    forward = exchange(False, fsend, frecv, fs_sem, fr_sem)
    backward = exchange(True, bsend, brecv, bs_sem, br_sem)

    def row_copy(half, r):
        slot = half * n_norm + r
        return pltpu.make_async_remote_copy(
            src_ref=rsend.at[half], dst_ref=rrecv.at[slot], send_sem=rs_sem.at[slot], recv_sem=rr_sem.at[slot],
            device_id=norm_peer(r), device_id_type=MESH,
        )

    forward[0]()

    loads[2].wait()
    t_index = lax.broadcasted_iota(jnp.int32, (chunk, chunk), 0)
    s_index = lax.broadcasted_iota(jnp.int32, (chunk, chunk), 1)
    for c in range(count):
        column = jnp.broadcast_to(run_t[:, c : c + 1], (chunk, chunk))
        fd[rows[c], :] = jnp.exp(column[:, 0:dim])
        gap = jnp.minimum(column - steps[c : c + 1, :], 0.0)
        weights = jnp.where(t_index >= s_index, jnp.exp(gap), 0.0)
        table[c] = weights
        scores = (mm(q[rows[c], :], k[rows[c], :], NT) * weights).astype(BF)
        wq[c] = scores
        attn[rows[c], :] = mm(scores, v[rows[c], :], NN)
    forward[1]()
    loads[3].wait()
    loads[4].wait()
    loads[5].wait()
    gain = gain_ref[...]
    for c in range(count):
        prob = jax.nn.sigmoid(gi[rows[c], :].astype(F32))
        gate[rows[c], :] = prob
        signal[rows[c], :] = go[rows[c], :].astype(F32) * prob * gain

    for c in range(count):
        high, low = split(jnp.transpose(q[rows[c], :].astype(F32) * fd[rows[c], :]))
        turned_q[c, 0:dim, :] = high
        turned_q[c, dim : 2 * dim, :] = low

    forward[2]()

    state = acc[...]
    ones = jnp.ones((8, dim), BF)
    halves = rsend.shape[0]
    per = count // halves
    for c in range(count):
        half, part = c // per, pl.ds((c % per) * chunk, chunk)
        high, low = split(state)
        ent[c, :, 0:dim] = high
        ent[c, :, dim : 2 * dim] = low
        both = mm(q[rows[c], :], ent[c], NN)
        full = attn[rows[c], :] + fd[rows[c], :] * (both[:, 0:dim] + both[:, dim : 2 * dim])
        attn[rows[c], :] = full
        rsend[half, 0:1, part] = mm(ones, (full * full).astype(BF), NT)[0:1, :]
        rsend[half, 1:2, part] = mm(ones, (signal[rows[c], :] * full).astype(BF), NT)[0:1, :]
        if c + 1 < count:
            state = jnp.exp(ends[c]) * state + upd[c]
        if c % per == per - 1:
            for r in range(1, n_norm):
                row_copy(half, r).start()

    coef[...] = jnp.zeros_like(coef)
    seen = [None] * count
    for c in range(count):
        half = c // per
        if c % per == 0:
            sums = rsend[half]
            for r in range(1, n_norm):
                row_copy(half, r).wait_recv()
                sums = sums + rrecv[half * n_norm + r]
            inv = lax.rsqrt(sums[0:1, :] / width + epsilon)
            here = pl.ds(half * per * chunk, per * chunk)
            coef[0:1, here] = inv
            coef[1:2, here] = inv * inv * (sums[1:2, :] / width)
        turned = jnp.transpose(coef[:, rows[c]])
        inv_b = jnp.broadcast_to(turned[:, 0:1], (chunk, dim))
        along_b = jnp.broadcast_to(turned[:, 1:2], (chunk, dim))
        full = attn[rows[c], :]
        grad = (inv_b * (signal[rows[c], :] - full * along_b)).astype(BF)
        g[rows[c], :] = grad
        inv_cols[rows[c], :] = inv_b
        both = mm(turned_q[c], grad, NN)
        seen[c] = both[0:dim, :] + both[dim : 2 * dim, :]
        upd[c] = seen[c]
    local = None
    for c in range(count - 1, -1, -1):
        local = seen[c] if local is None else jnp.exp(ends[c]) * local + seen[c]
    bsend[0:dim, :] = local
    bsend[dim : dim + EXTRA, :] = jnp.broadcast_to(total, (EXTRA, dim))
    backward[0]()

    for c in range(count):
        grad = g[rows[c], :]
        dv = (mm(grad, v[rows[c], :], NT) * table[c]).astype(BF)
        high = mm(grad, ent[c, :, 0:dim], NT)
        low = mm(grad, ent[c, :, dim : 2 * dim], NT)
        gq[rows[c], :] = (
            mm(dv, k[rows[c], :], NN) + fd[rows[c], :] * (high + low)
        ).astype(BF)
        gkl[rows[c], :] = mm(dv, q[rows[c], :], TN)
        gvl[rows[c], :] = mm(wq[c], grad, TN)
    backward[1]()
    for c in range(count):
        prob = gate[rows[c], :]
        out = attn[rows[c], :] * inv_cols[rows[c], :] * gain * prob
        lo[rows[c], :] = out.astype(BF)
        gg[rows[c], :] = (go[rows[c], :].astype(F32) * out * (1.0 - prob)).astype(BF)

    backward[2]()

    state = acc[...]
    for c in range(count - 1, -1, -1):
        high, low = split(state)
        wide = jnp.concatenate([high, low], axis=1)
        tall = jnp.concatenate([high, low], axis=0)
        fall = tail[rows[c], :]
        vc = v[rows[c], :]
        kc = k[rows[c], :]
        from_v = mm(vc, tall, NT)
        from_k = mm(kc, wide, NN)
        gk[rows[c], :] = (gkl[rows[c], :] + fall * (from_v[:, 0:dim] + from_v[:, dim : 2 * dim])).astype(BF)
        gv[rows[c], :] = (gvl[rows[c], :] + fall * (from_k[:, 0:dim] + from_k[:, dim : 2 * dim])).astype(BF)
        if c > 0:
            state = jnp.exp(ends[c]) * state + upd[c]

    forward[3]()
    backward[3]()
    for half in range(halves):
        for r in range(1, n_norm):
            row_copy(half, r).wait_send()


def hand_out(*refs):
    copies = [pltpu.make_async_copy(refs[i], refs[5 + i], refs[10].at[i]) for i in range(5)]
    for copy in copies:
        copy.start()
    for copy in copies:
        copy.wait()


def on_device(n_ctx, n_sec, n_exp, queries, key_rows, value_rows, gate_input, norm_gain, log_decay, grad_output):
    length, dim = queries.shape
    assert log_decay.shape[0] == 1
    chunk = min(256, length)
    count = length // chunk
    assert count * chunk == length and count <= 8
    n_norm = n_sec * n_exp
    halves = 2 if count % 2 == 0 else 1
    any_spec = pl.BlockSpec(memory_space=pl.ANY)
    hbm_spec = pl.BlockSpec(memory_space=pltpu.HBM)
    block = lambda dtype: pltpu.VMEM((length, dim), dtype)
    sem = lambda n: pltpu.SemaphoreType.DMA((n,))
    results = pl.pallas_call(
        partial(kernel, (n_ctx, n_sec, n_exp, chunk)),
        out_shape=[pltpu.VMEM((length, dim), BF)] * 5,
        in_specs=[hbm_spec] * 7,
        out_specs=[pl.BlockSpec(memory_space=pltpu.VMEM)] * 5,
        scratch_shapes=[block(BF)] * 5
        + [
            pltpu.VMEM((1, dim), F32),
            pltpu.VMEM((1, length), F32),
            pltpu.VMEM((8, chunk), F32),
            block(F32),
            block(F32),
            pltpu.VMEM((count, chunk, chunk), F32),
            pltpu.VMEM((count, chunk, chunk), BF),
            block(F32),
            block(F32),
            block(F32),
            pltpu.VMEM((count, dim, dim), F32),
            pltpu.VMEM((count, dim, 2 * dim), BF),
            block(BF),
            block(F32),
            block(F32),
            pltpu.VMEM((count, 2 * dim, chunk), BF),
            block(F32),
            pltpu.VMEM((dim + EXTRA, dim), F32),
            pltpu.VMEM((n_ctx, dim + EXTRA, dim), F32),
            pltpu.VMEM((dim + EXTRA, dim), F32),
            pltpu.VMEM((n_ctx, dim + EXTRA, dim), F32),
            pltpu.VMEM((dim, dim), F32),
            pltpu.VMEM((halves, 2, length // halves), F32),
            pltpu.VMEM((halves * n_norm, 2, length // halves), F32),
            pltpu.VMEM((8, length), F32),
            sem(7), sem(n_ctx), sem(n_ctx), sem(n_ctx), sem(n_ctx), sem(halves * n_norm), sem(halves * n_norm),
        ],
        compiler_params=pltpu.CompilerParams(
            collective_id=0, has_side_effects=True, vmem_limit_bytes=48 * 1024 * 1024
        ),
    )(*[
        pltpu.with_memory_space_constraint(x, pltpu.HBM)
        for x in (queries, key_rows, value_rows, gate_input, grad_output, norm_gain.reshape(1, dim), log_decay)
    ])
    return pl.pallas_call(
        hand_out,
        out_shape=[jax.ShapeDtypeStruct((length, dim), BF)] * 5,
        in_specs=[any_spec] * 5,
        out_specs=[hbm_spec] * 5,
        scratch_shapes=[sem(5)],
        compiler_params=pltpu.CompilerParams(vmem_limit_bytes=2 * 1024 * 1024),
    )(*[pltpu.with_memory_space_constraint(x, pltpu.VMEM) for x in results])


def solution(mesh):
    rows = P("ctx", ("section", "exp"))
    in_specs = (rows, rows, rows, rows, P(("section", "exp")), P(("section", "exp"), "ctx"), rows)
    call = partial(on_device, mesh.shape["ctx"], mesh.shape["section"], mesh.shape["exp"])

    def run(*args):
        return tuple(call(*args))

    return jax.shard_map(run, mesh=mesh, in_specs=in_specs, out_specs=(rows,) * 5, check_vma=False)
```

```python
from functools import partial

import jax
import jax.numpy as jnp
from jax import lax
from jax.experimental import pallas as pl
from jax.experimental.pallas import tpu as pltpu
from jax.sharding import PartitionSpec as P

MESH = pl.DeviceIdType.MESH
BF = jnp.bfloat16
F32 = jnp.float32
epsilon = 1e-06
EXTRA = 8

NN = (((1,), (0,)), ((), ()))
NT = (((1,), (1,)), ((), ()))
TN = (((0,), (0,)), ((), ()))


def mm(a, b, dims):
    return lax.dot_general(a, b, dims, preferred_element_type=F32)


def pieces(dim):
    return ((0, dim // 2), (dim // 2, dim - dim // 2 + EXTRA))


def split(x):
    high = x.astype(BF)
    return high, (x - high.astype(F32)).astype(BF)


def prefix_rows(x):
    size = x.shape[1]
    first = lax.broadcasted_iota(jnp.int32, (size, size), 0)
    last = lax.broadcasted_iota(jnp.int32, (size, size), 1)
    upto = jnp.where(first <= last, 1.0, 0.0).astype(BF)
    high, low = split(x)
    rest = (x - high.astype(F32) - low.astype(F32)).astype(BF)
    return mm(high, upto, NN) + (mm(low, upto, NN) + mm(rest, upto, NN))


def kernel(
    sizes,
    q_h, k_h, v_h, gi_h, go_h, gain_h, ld_h,
    lo, gq, gk, gv, gg,
    q, k, v, gi, go,
    gain_ref, ld_ref, steps, fd, tail, table, wq, attn, signal, gate, upd, ent, g, gkl, gvl, turned_q, inv_cols,
    fsend, frecv, bsend, brecv, acc, rsend, rrecv, coef,
    in_sem, fs_sem, fr_sem, bs_sem, br_sem, rs_sem, rr_sem,
):
    n_ctx, n_sec, n_exp, chunk = sizes
    n_norm = n_sec * n_exp
    length, dim = q.shape
    count = length // chunk
    me = lax.axis_index("ctx")
    pair = 2 if n_ctx % 2 == 0 else 1
    n_row = n_ctx // pair
    row, core = lax.div(me, pair), lax.rem(me, pair)
    sec = lax.axis_index("section")
    ex = lax.axis_index("exp")
    mine = sec * n_exp + ex
    width = float(dim * n_norm)

    def norm_peer(r):
        other = lax.rem(mine + r, n_norm)
        return {"section": lax.div(other, n_exp), "exp": lax.rem(other, n_exp)}

    loads = [
        pltpu.make_async_copy(src, dst, in_sem.at[i])
        for i, (src, dst) in enumerate(
            ((k_h, k), (v_h, v), (q_h, q), (gi_h, gi), (go_h, go), (gain_h, gain_ref), (ld_h, ld_ref))
        )
    ]
    for i in (6, 0, 1, 2, 3, 4, 5):
        loads[i].start()

    barrier = pltpu.get_barrier_semaphore()
    for r in range(1, n_row):
        other = lax.rem(row + r, n_row) * pair + core
        pl.semaphore_signal(barrier, inc=1, device_id={"ctx": other}, device_id_type=MESH)
    if pair == 2:
        twin = row * pair + 1 - core
        pl.semaphore_signal(barrier, inc=1, device_id={"ctx": twin}, device_id_type=MESH)
    for r in range(1, n_norm):
        pl.semaphore_signal(barrier, inc=1, device_id=norm_peer(r), device_id_type=MESH)

    rows = [pl.ds(c * chunk, chunk) for c in range(count)]

    steps[...] = jnp.zeros_like(steps)
    loads[6].wait()
    for c in range(count):
        steps[c : c + 1, :] = ld_ref[:, c * chunk : (c + 1) * chunk]
    run = prefix_rows(steps[...])
    steps[...] = run
    run_t = jnp.transpose(run)
    ends = [run[c : c + 1, chunk - 1 : chunk] for c in range(count)]
    for c in range(count):
        column = jnp.broadcast_to(run_t[:, c : c + 1], (chunk, dim))
        tail[rows[c], :] = jnp.exp(ends[c] - column)

    loads[0].wait()
    loads[1].wait()
    local = None
    total = None
    for c in range(count):
        high, low = split(k[rows[c], :].astype(F32) * tail[rows[c], :])
        vc = v[rows[c], :]
        update = mm(high, vc, TN) + mm(low, vc, TN)
        upd[c] = update
        local = update if local is None else jnp.exp(ends[c]) * local + update
        total = ends[c] if total is None else total + ends[c]
    fsend[0:dim, :] = local
    fsend[dim : dim + EXTRA, :] = jnp.broadcast_to(total, (EXTRA, dim))

    pl.semaphore_wait(barrier, n_row - 1 + pair - 1 + n_norm - 1)

    def exchange(reverse, send, recv, s_sem, r_sem):
        y, c = (n_row - 1 - row, pair - 1 - core) if reverse else (row, core)

        def to(y_to, c_to):
            if reverse:
                y_to, c_to = n_row - 1 - y_to, pair - 1 - c_to
            return {"ctx": y_to * pair + c_to}

        def copy(src, slot, target, part):
            rows_of = pl.ds(*pieces(dim)[part])
            return pltpu.make_async_remote_copy(
                src_ref=src.at[rows_of], dst_ref=recv.at[slot, rows_of],
                send_sem=s_sem.at[2 * slot + part], recv_sem=r_sem.at[2 * slot + part],
                device_id=target, device_id_type=MESH,
            )

        def direct(d, part):
            return copy(send, d * pair, to(lax.rem(y + d, n_row), c), part)

        def relay(d, part):
            return copy(recv.at[d * pair], d * pair + 1, to(y, 1 - c), part)

        def neighbour(part):
            return copy(send, 1, to(y, 1 - c), part)

        def start():
            for d in range(1, n_row):
                @pl.when(y + d < n_row)
                def _(d=d):
                    for part in range(2):
                        direct(d, part).start()
            if pair == 2:
                @pl.when(c == 0)
                def _():
                    for part in range(2):
                        neighbour(part).start()

        def pass_on():
            for d in range(1, n_row):
                @pl.when(y >= d)
                def _(d=d):
                    for part in range(2):
                        direct(d, part).wait_recv()
                        if pair == 2:
                            relay(d, part).start()

        def join(slot):
            acc[...] = jnp.exp(recv[slot, dim : dim + 1, :]) * acc[...] + recv[slot, 0:dim, :]

        def collect():
            acc[...] = jnp.zeros_like(acc)
            for d in range(n_row - 1, 0, -1):
                @pl.when(y >= d)
                def _(d=d):
                    if pair == 2:
                        for part in range(2):
                            relay(d, part).wait_recv()
                        join(d * pair + c)
                        join(d * pair + 1 - c)
                    else:
                        join(d)
            if pair == 2:
                @pl.when(c == 1)
                def _():
                    for part in range(2):
                        neighbour(part).wait_recv()
                    join(1)

        def finish():
            for d in range(1, n_row):
                @pl.when(y + d < n_row)
                def _(d=d):
                    for part in range(2):
                        direct(d, part).wait_send()
                if pair == 2:
                    @pl.when(y >= d)
                    def _(d=d):
                        for part in range(2):
                            relay(d, part).wait_send()
            if pair == 2:
                @pl.when(c == 0)
                def _():
                    for part in range(2):
                        neighbour(part).wait_send()

        return start, pass_on, collect, finish

    forward = exchange(False, fsend, frecv, fs_sem, fr_sem)
    backward = exchange(True, bsend, brecv, bs_sem, br_sem)

    def row_copy(half, r):
        slot = half * n_norm + r
        return pltpu.make_async_remote_copy(
            src_ref=rsend.at[half], dst_ref=rrecv.at[slot], send_sem=rs_sem.at[slot], recv_sem=rr_sem.at[slot],
            device_id=norm_peer(r), device_id_type=MESH,
        )

    forward[0]()

    loads[2].wait()
    t_index = lax.broadcasted_iota(jnp.int32, (chunk, chunk), 0)
    s_index = lax.broadcasted_iota(jnp.int32, (chunk, chunk), 1)
    for c in range(count):
        column = jnp.broadcast_to(run_t[:, c : c + 1], (chunk, chunk))
        fd[rows[c], :] = jnp.exp(column[:, 0:dim])
        gap = jnp.minimum(column - steps[c : c + 1, :], 0.0)
        weights = jnp.where(t_index >= s_index, jnp.exp(gap), 0.0)
        table[c] = weights
        scores = (mm(q[rows[c], :], k[rows[c], :], NT) * weights).astype(BF)
        wq[c] = scores
        attn[rows[c], :] = mm(scores, v[rows[c], :], NN)
    forward[1]()
    loads[3].wait()
    loads[4].wait()
    loads[5].wait()
    gain = gain_ref[...]
    for c in range(count):
        prob = jax.nn.sigmoid(gi[rows[c], :].astype(F32))
        gate[rows[c], :] = prob
        signal[rows[c], :] = go[rows[c], :].astype(F32) * prob * gain

    for c in range(count):
        high, low = split(jnp.transpose(q[rows[c], :].astype(F32) * fd[rows[c], :]))
        turned_q[c, 0:dim, :] = high
        turned_q[c, dim : 2 * dim, :] = low

    forward[2]()

    state = acc[...]
    ones = jnp.ones((8, dim), BF)
    halves = rsend.shape[0]
    per = count // halves
    for c in range(count):
        half, part = c // per, pl.ds((c % per) * chunk, chunk)
        high, low = split(state)
        ent[c, :, 0:dim] = high
        ent[c, :, dim : 2 * dim] = low
        both = mm(q[rows[c], :], ent[c], NN)
        full = attn[rows[c], :] + fd[rows[c], :] * (both[:, 0:dim] + both[:, dim : 2 * dim])
        attn[rows[c], :] = full
        rsend[half, 0:1, part] = mm(ones, (full * full).astype(BF), NT)[0:1, :]
        rsend[half, 1:2, part] = mm(ones, (signal[rows[c], :] * full).astype(BF), NT)[0:1, :]
        if c + 1 < count:
            state = jnp.exp(ends[c]) * state + upd[c]
        if c % per == per - 1:
            for r in range(1, n_norm):
                row_copy(half, r).start()

    coef[...] = jnp.zeros_like(coef)
    seen = [None] * count
    for c in range(count):
        half = c // per
        if c % per == 0:
            sums = rsend[half]
            for r in range(1, n_norm):
                row_copy(half, r).wait_recv()
                sums = sums + rrecv[half * n_norm + r]
            inv = lax.rsqrt(sums[0:1, :] / width + epsilon)
            here = pl.ds(half * per * chunk, per * chunk)
            coef[0:1, here] = inv
            coef[1:2, here] = inv * inv * (sums[1:2, :] / width)
        turned = jnp.transpose(coef[:, rows[c]])
        inv_b = jnp.broadcast_to(turned[:, 0:1], (chunk, dim))
        along_b = jnp.broadcast_to(turned[:, 1:2], (chunk, dim))
        full = attn[rows[c], :]
        grad = (inv_b * (signal[rows[c], :] - full * along_b)).astype(BF)
        g[rows[c], :] = grad
        inv_cols[rows[c], :] = inv_b
        both = mm(turned_q[c], grad, NN)
        seen[c] = both[0:dim, :] + both[dim : 2 * dim, :]
        upd[c] = seen[c]
    local = None
    for c in range(count - 1, -1, -1):
        local = seen[c] if local is None else jnp.exp(ends[c]) * local + seen[c]
    bsend[0:dim, :] = local
    bsend[dim : dim + EXTRA, :] = jnp.broadcast_to(total, (EXTRA, dim))
    backward[0]()

    for c in range(count):
        grad = g[rows[c], :]
        dv = (mm(grad, v[rows[c], :], NT) * table[c]).astype(BF)
        high = mm(grad, ent[c, :, 0:dim], NT)
        low = mm(grad, ent[c, :, dim : 2 * dim], NT)
        gq[rows[c], :] = (
            mm(dv, k[rows[c], :], NN) + fd[rows[c], :] * (high + low)
        ).astype(BF)
        gkl[rows[c], :] = mm(dv, q[rows[c], :], TN)
        gvl[rows[c], :] = mm(wq[c], grad, TN)
    backward[1]()
    for c in range(count):
        prob = gate[rows[c], :]
        out = attn[rows[c], :] * inv_cols[rows[c], :] * gain * prob
        lo[rows[c], :] = out.astype(BF)
        gg[rows[c], :] = (go[rows[c], :].astype(F32) * out * (1.0 - prob)).astype(BF)

    backward[2]()

    state = acc[...]
    for c in range(count - 1, -1, -1):
        high, low = split(state)
        wide = jnp.concatenate([high, low], axis=1)
        tall = jnp.concatenate([high, low], axis=0)
        fall = tail[rows[c], :]
        vc = v[rows[c], :]
        kc = k[rows[c], :]
        from_v = mm(vc, tall, NT)
        from_k = mm(kc, wide, NN)
        gk[rows[c], :] = (gkl[rows[c], :] + fall * (from_v[:, 0:dim] + from_v[:, dim : 2 * dim])).astype(BF)
        gv[rows[c], :] = (gvl[rows[c], :] + fall * (from_k[:, 0:dim] + from_k[:, dim : 2 * dim])).astype(BF)
        if c > 0:
            state = jnp.exp(ends[c]) * state + upd[c]

    forward[3]()
    backward[3]()
    for half in range(halves):
        for r in range(1, n_norm):
            row_copy(half, r).wait_send()


def hand_out(*refs):
    copies = [pltpu.make_async_copy(refs[i], refs[5 + i], refs[10].at[i]) for i in range(5)]
    for copy in copies:
        copy.start()
    for copy in copies:
        copy.wait()


def on_device(n_ctx, n_sec, n_exp, queries, key_rows, value_rows, gate_input, norm_gain, log_decay, grad_output):
    length, dim = queries.shape
    assert log_decay.shape[0] == 1
    chunk = min(256, length)
    count = length // chunk
    assert count * chunk == length and count <= 8
    n_norm = n_sec * n_exp
    halves = 2 if count % 2 == 0 else 1
    any_spec = pl.BlockSpec(memory_space=pl.ANY)
    hbm_spec = pl.BlockSpec(memory_space=pltpu.HBM)
    block = lambda dtype: pltpu.VMEM((length, dim), dtype)
    sem = lambda n: pltpu.SemaphoreType.DMA((n,))
    results = pl.pallas_call(
        partial(kernel, (n_ctx, n_sec, n_exp, chunk)),
        out_shape=[pltpu.VMEM((length, dim), BF)] * 5,
        in_specs=[hbm_spec] * 7,
        out_specs=[pl.BlockSpec(memory_space=pltpu.VMEM)] * 5,
        scratch_shapes=[block(BF)] * 5
        + [
            pltpu.VMEM((1, dim), F32),
            pltpu.VMEM((1, length), F32),
            pltpu.VMEM((8, chunk), F32),
            block(F32),
            block(F32),
            pltpu.VMEM((count, chunk, chunk), F32),
            pltpu.VMEM((count, chunk, chunk), BF),
            block(F32),
            block(F32),
            block(F32),
            pltpu.VMEM((count, dim, dim), F32),
            pltpu.VMEM((count, dim, 2 * dim), BF),
            block(BF),
            block(F32),
            block(F32),
            pltpu.VMEM((count, 2 * dim, chunk), BF),
            block(F32),
            pltpu.VMEM((dim + EXTRA, dim), F32),
            pltpu.VMEM((n_ctx, dim + EXTRA, dim), F32),
            pltpu.VMEM((dim + EXTRA, dim), F32),
            pltpu.VMEM((n_ctx, dim + EXTRA, dim), F32),
            pltpu.VMEM((dim, dim), F32),
            pltpu.VMEM((halves, 2, length // halves), F32),
            pltpu.VMEM((halves * n_norm, 2, length // halves), F32),
            pltpu.VMEM((8, length), F32),
            sem(7), sem(2 * n_ctx), sem(2 * n_ctx), sem(2 * n_ctx), sem(2 * n_ctx), sem(halves * n_norm), sem(halves * n_norm),
        ],
        compiler_params=pltpu.CompilerParams(
            collective_id=0, has_side_effects=True, vmem_limit_bytes=48 * 1024 * 1024
        ),
    )(*[
        pltpu.with_memory_space_constraint(x, pltpu.HBM)
        for x in (queries, key_rows, value_rows, gate_input, grad_output, norm_gain.reshape(1, dim), log_decay)
    ])
    return pl.pallas_call(
        hand_out,
        out_shape=[jax.ShapeDtypeStruct((length, dim), BF)] * 5,
        in_specs=[any_spec] * 5,
        out_specs=[hbm_spec] * 5,
        scratch_shapes=[sem(5)],
        compiler_params=pltpu.CompilerParams(vmem_limit_bytes=2 * 1024 * 1024),
    )(*[pltpu.with_memory_space_constraint(x, pltpu.VMEM) for x in results])


def solution(mesh):
    rows = P("ctx", ("section", "exp"))
    in_specs = (rows, rows, rows, rows, P(("section", "exp")), P(("section", "exp"), "ctx"), rows)
    call = partial(on_device, mesh.shape["ctx"], mesh.shape["section"], mesh.shape["exp"])

    def run(*args):
        return tuple(call(*args))

    return jax.shard_map(run, mesh=mesh, in_specs=in_specs, out_specs=(rows,) * 5, check_vma=False)
```
